256 devices in a mesh: dp: 16 (over z, core), seq: 16 (over x, y).
Axes of the slice: x: 4, y: 4, z: 8, core: 2. Of those that a mesh axis runs over, the one named last changes fastest.
Arguments:
- gated_part: bfloat16 [16, 3072, 4096], P('dp', 'seq'), may hold values from -6 to 6
- mixed_part: bfloat16 [16, 3072, 4096], P('dp', 'seq'), may hold values from -400 to 400
- out_grad: bfloat16 [16, 3072, 4096], P('dp', 'seq'), may hold values from -6 to 6
- norm_gain: float32 [4096], replicated, may hold values from 0.1 to 1.9
- mix_bias: float32 [3072], replicated, may hold values from -4 to 4
- token_mixing_weight: bfloat16 [18, 128, 128], replicated, may hold values from -0.125 to 0.125
- stride_cols: int32 [24, 2], replicated, may hold values from -1 to 7, as said below
Outputs:
- gated_grad: bfloat16 [16, 3072, 4096], P('dp', 'seq')
- value_grad: bfloat16 [16, 3072, 4096], P('dp', 'seq')
- weight_grad: float32 [18, 128, 128], replicated
- gain_grad: float32 [4096], replicated
- bias_grad: float32 [3072], P('seq')
The draws below stay inside these ranges and needn't reach their ends.
Inputs may be any that keep to these rules, and one draw needn't show every extreme that they name: stride_cols[i, s] is -1 for row blocks i < 16, and otherwise a column block from 0 to i - 16; -1 means no strided block; stride_cols[23, 0] is 7.
All inputs are finite; a program needn't handle non-finite values.
Results may differ from the reference program's by a relative error of at most 0.0085.
Values may be sent and summed in bfloat16 or wider, within the bound.
A program may use at most 128 MiB of HBM per device.

```python
import math
import jax
import jax.numpy as jnp
from jax import lax

HALF_FEATURES = 4096
SEQUENCE_LENGTH = 3072
MIXING_BLOCK = 128
BAND_BLOCKS = 16
NSTR = 2
BATCH = 16
NB = 24
WEIGHT_SLOTS = 18


def draw_mixed_part(key, part):
    key_base, key_rows, key_cols = jax.random.split(key, 3)
    full_shape = (BATCH, SEQUENCE_LENGTH, HALF_FEATURES)
    base_draw = jax.random.normal(key_base, full_shape, jnp.float32)
    base_draw = jnp.clip(base_draw, -4.0, 4.0)
    row_scale = jnp.exp(jax.random.uniform(key_rows, (BATCH, SEQUENCE_LENGTH, 1), jnp.float32, 0.0, math.log(10.0)))
    col_scale = jnp.exp(jax.random.uniform(key_cols, (1, 1, HALF_FEATURES), jnp.float32, 0.0, math.log(10.0)))
    return (base_draw * row_scale * col_scale).astype(jnp.bfloat16)


def draw_stride_cols(key, part):
    row_idx = jnp.arange(NB, dtype=jnp.int32)[:, None]
    slot_idx = jnp.arange(NSTR, dtype=jnp.int32)[None, :]
    pick_span = jnp.maximum(row_idx - BAND_BLOCKS + 1, 1)
    raw_pick = jax.random.randint(key, (NB, NSTR), 0, 1 << 20, dtype=jnp.int32)
    chosen = raw_pick % pick_span
    chosen = jnp.where((row_idx == NB - 1) & (slot_idx == 0), pick_span - 1, chosen)
    return jnp.where(row_idx >= BAND_BLOCKS, chosen, -1).astype(jnp.int32)


def level_of(own_key, extent, shards, smallest, largest):
    loudness = 1.0
    for dim, parts in shards:
        draws = jax.random.uniform(jax.random.fold_in(jax.random.fold_in(own_key, 6), dim), (parts,), jnp.float32, smallest / len(shards), largest / len(shards))
        loudness = loudness * jnp.repeat(jnp.exp(draws), extent[dim] // parts).reshape((-1,) + (1,) * (len(extent) - 1 - dim))
    return loudness


def normal_values(own_key, extent, spread, most, cuts=(), kind=jnp.bfloat16):
    array = jax.random.normal(own_key, extent, jnp.float32) * spread
    if len(cuts) > 0:
        array = level_of(own_key, extent, cuts, -0.22, 0.18) * array
    return jnp.clip(array, min=-most, max=most).astype(kind)


def setup_inputs(seed: int = 0) -> dict:
    key_list = jax.random.split(jax.random.key(seed), 8)
    gated_part = normal_values(key_list[0], (BATCH, SEQUENCE_LENGTH, HALF_FEATURES), 1.0, 6.0, ((0, 16), (1, 16)))
    mixed_part = draw_mixed_part(jax.random.fold_in(key_list[7], 71), 0)
    out_grad = normal_values(key_list[2], (BATCH, SEQUENCE_LENGTH, HALF_FEATURES), 1.0, 6.0, ((0, 16), (1, 16)))
    norm_gain = jnp.clip(1.0 + 0.18 * jax.random.normal(key_list[3], (HALF_FEATURES,), jnp.float32), 0.1, 1.9)
    mix_bias = normal_values(key_list[4], (SEQUENCE_LENGTH,), 1.0, 4.0, (), jnp.float32)
    token_mixing_weight = normal_values(key_list[5], (WEIGHT_SLOTS, MIXING_BLOCK, MIXING_BLOCK), (MIXING_BLOCK * BAND_BLOCKS) ** -0.5, 0.125)
    stride_cols = draw_stride_cols(jax.random.fold_in(key_list[7], 71), 0)
    return {"gated_part": gated_part, "mixed_part": mixed_part, "out_grad": out_grad, "norm_gain": norm_gain, "mix_bias": mix_bias, "token_mixing_weight": token_mixing_weight, "stride_cols": stride_cols}


EPS = 1e-05

def slot_mask(shape):
    slot_idx = lax.broadcasted_iota(jnp.int32, shape, 0)
    row_idx = lax.broadcasted_iota(jnp.int32, shape, 1)
    col_idx = lax.broadcasted_iota(jnp.int32, shape, 2)
    return (slot_idx > 0) | (row_idx >= col_idx)

def shift_down(blocks, offset):
    zero_pad = jnp.zeros((offset,) + blocks.shape[1:], blocks.dtype)
    return jnp.concatenate([zero_pad, blocks[:blocks.shape[0] - offset]], axis=0)

def shift_up(blocks, offset):
    zero_pad = jnp.zeros((offset,) + blocks.shape[1:], blocks.dtype)
    return jnp.concatenate([blocks[offset:], zero_pad], axis=0)

def reference(gated_part, mixed_part, out_grad, norm_gain, mix_bias, token_mixing_weight, stride_cols):
    keep_mask = slot_mask(token_mixing_weight.shape)
    weights = jnp.where(keep_mask, token_mixing_weight.astype(jnp.float32), jnp.zeros((), jnp.float32))
    valid_rows = stride_cols >= 0
    safe_cols = jnp.maximum(stride_cols, 0).astype(jnp.int32)

    def one_sequence(carry, inputs):
        weight_acc, gain_acc, bias_acc = carry
        gated_seq, value_seq, grad_seq = inputs
        values = value_seq.astype(jnp.float32)
        row_mean = lax.optimization_barrier(jnp.mean(values, axis=1, keepdims=True))
        centered = values - row_mean
        row_var = lax.optimization_barrier(jnp.mean(centered * centered, axis=1, keepdims=True))
        inv_std = lax.rsqrt(row_var + EPS)
        norm_hat = centered * inv_std
        normed = (norm_hat * norm_gain).astype(jnp.bfloat16)
        blocks = normed.astype(jnp.float32).reshape(NB, MIXING_BLOCK, HALF_FEATURES)
        mixed_sum = jnp.zeros((NB, MIXING_BLOCK, HALF_FEATURES), jnp.float32)
        for offset in range(BAND_BLOCKS):
            mixed_sum = mixed_sum + jnp.einsum('ab,nbc->nac', weights[offset], shift_down(blocks, offset))
        picked_all = []
        for strided in range(NSTR):
            picked = jnp.where(valid_rows[:, strided, None, None], blocks[safe_cols[:, strided]], jnp.zeros((), jnp.float32))
            picked_all.append(picked)
            mixed_sum = mixed_sum + jnp.einsum('ab,nbc->nac', weights[BAND_BLOCKS + strided], picked)
        mixed_sum = mixed_sum.reshape(SEQUENCE_LENGTH, HALF_FEATURES) + mix_bias[:, None]
        mixed16 = mixed_sum.astype(jnp.bfloat16)
        grad_f32 = grad_seq.astype(jnp.float32)
        gated_grad = (grad_f32 * mixed16.astype(jnp.float32)).astype(jnp.bfloat16)
        dmix16 = (grad_f32 * gated_seq.astype(jnp.float32)).astype(jnp.bfloat16)
        bias_part = lax.optimization_barrier(jnp.sum(dmix16.astype(jnp.float32), axis=1))
        dblocks = dmix16.astype(jnp.float32).reshape(NB, MIXING_BLOCK, HALF_FEATURES)
        dnorm = jnp.zeros((NB, MIXING_BLOCK, HALF_FEATURES), jnp.float32)
        slot_grads = []
        for offset in range(BAND_BLOCKS):
            dnorm = dnorm + jnp.einsum('ab,nac->nbc', weights[offset], shift_up(dblocks, offset))
            slot_grads.append(jnp.einsum('nac,nbc->ab', dblocks, shift_down(blocks, offset)))
        for strided in range(NSTR):
            slot_grads.append(jnp.einsum('nac,nbc->ab', dblocks, picked_all[strided]))
            scatter_term = jnp.einsum('ab,nac->nbc', weights[BAND_BLOCKS + strided], dblocks)
            scatter_term = jnp.where(valid_rows[:, strided, None, None], scatter_term, jnp.zeros((), jnp.float32))
            dnorm = dnorm.at[safe_cols[:, strided]].add(scatter_term)
        slot_grad = jnp.where(keep_mask, jnp.stack(slot_grads), jnp.zeros((), jnp.float32))
        dnorm16 = dnorm.reshape(SEQUENCE_LENGTH, HALF_FEATURES).astype(jnp.bfloat16)
        dnorm_f32 = dnorm16.astype(jnp.float32)
        hat_grad = dnorm_f32 * norm_gain
        value_grad = inv_std * (hat_grad - lax.optimization_barrier(jnp.mean(hat_grad, axis=1, keepdims=True)) - norm_hat * lax.optimization_barrier(jnp.mean(hat_grad * norm_hat, axis=1, keepdims=True)))
        gain_part = lax.optimization_barrier(jnp.sum(dnorm_f32 * norm_hat, axis=0))
        new_carry = (weight_acc + slot_grad, gain_acc + gain_part, bias_acc + bias_part)
        return (new_carry, (gated_grad, value_grad.astype(jnp.bfloat16)))
    initialize = (jnp.zeros((WEIGHT_SLOTS, MIXING_BLOCK, MIXING_BLOCK), jnp.float32), jnp.zeros((HALF_FEATURES,), jnp.float32), jnp.zeros((SEQUENCE_LENGTH,), jnp.float32))
    carry, outputs = lax.scan(one_sequence, initialize, (gated_part, mixed_part, out_grad))
    weight_acc, gain_acc, bias_acc = carry
    gated_grad, value_grad = outputs
    weight_grad = weight_acc / math.sqrt(BATCH * SEQUENCE_LENGTH * HALF_FEATURES)
    gain_grad = gain_acc / math.sqrt(BATCH * SEQUENCE_LENGTH)
    bias_grad = bias_acc / math.sqrt(BATCH * HALF_FEATURES)
    return (gated_grad, value_grad, weight_grad, gain_grad, bias_grad)
```

```python
import math

import jax
import jax.numpy as jnp
from jax import lax
from jax.experimental import pallas as pl
from jax.experimental.pallas import tpu as pltpu
from jax.sharding import PartitionSpec as P

BLOCK = 128
BAND = 16
NSTR = 2
EPS = 1e-05
MESH = pl.DeviceIdType.MESH
F32 = jnp.float32
BF16 = jnp.bfloat16

OFFSETS = (
    (2, 2), (1, 2), (2, 1), (3, 2), (2, 3), (1, 1), (3, 3), (1, 3),
    (3, 1), (0, 2), (2, 0), (0, 1), (1, 0), (0, 3), (3, 0),
)

SEQ = 16
DP = 16
TOK = 192
FEAT = 4096
WIDTH = FEAT // SEQ
TOTAL = TOK * SEQ
GROUPS = TOTAL // (2 * BLOCK)
SPAN = (BAND + 1) * BLOCK
PAD = (BAND - 1) * BLOCK
SLOTS = BAND + NSTR
PIECE = SLOTS * BLOCK // DP
SUB = 16
REDUCERS = PIECE // SUB
CHUNK = 16

S_D, S_N, S_DN, S_MX, S_R1, S_R2, S_R2B, S_R3, S_BIAS, S_G1, S_G2 = range(11)
PHASES = 11
MIX_FIRST = 5


def rows(start, size):
    return pl.ds(pl.multiple_of(start, 16), size)


def lanes(start, size):
    return pl.ds(pl.multiple_of(start, 128), size)


def kernel(
    gated, value, grad, gain, bias, weights, cols,
    gated_grad, value_grad, weight_grad, gain_grad, bias_grad,
    u_ref, v_ref, g_ref, hat_ref, inv_ref,
    d_buf, n_buf, d_pad, n_pad, nt_pad, dn_all, mx_all, dn_back, mx_back,
    band, band_t, corner_t, wt_ref, picked, sums, slot_buf,
    r1, part, r2, r2b, r3_buf, r3, bias_acc, bias_all, g1_buf, g1, g2,
    in_sem, ss, rs,
):
    dp = lax.axis_index("dp")
    sq = lax.axis_index("seq")
    x, y = sq // 4, sq % 4

    def ahead(r):
        dx, dy = OFFSETS[r]
        return ((x + dx) % 4) * 4 + (y + dy) % 4

    def behind(r):
        dx, dy = OFFSETS[r]
        return ((x + 4 - dx) % 4) * 4 + (y + 4 - dy) % 4

    def to_seq(phase, r, src, dst):
        return pltpu.make_async_remote_copy(
            src_ref=src, dst_ref=dst, send_sem=ss.at[phase, r], recv_sem=rs.at[phase, r],
            device_id=(dp, ahead(r)), device_id_type=MESH,
        )

    def from_seq(phase, r, slot):
        pltpu.make_async_remote_copy(
            src_ref=slot, dst_ref=slot, send_sem=ss.at[phase, r], recv_sem=rs.at[phase, r],
            device_id=(dp, behind(r)), device_id_type=MESH,
        ).wait_recv()

    def to_dp(phase, r, src, dst):
        return pltpu.make_async_remote_copy(
            src_ref=src, dst_ref=dst, send_sem=ss.at[phase, r], recv_sem=rs.at[phase, r],
            device_id=((dp + r) % DP, sq), device_id_type=MESH,
        )

    def from_dp(phase, r, slot):
        pltpu.make_async_remote_copy(
            src_ref=slot, dst_ref=slot, send_sem=ss.at[phase, r], recv_sem=rs.at[phase, r],
            device_id=((dp + DP - r) % DP, sq), device_id_type=MESH,
        ).wait_recv()

    def other_dp(body):
        def step(r, carry):
            body(r)
            return carry

        lax.fori_loop(1, DP, step, 0)

    loads = [
        pltpu.make_async_copy(src, dst, in_sem.at[i])
        for i, (src, dst) in enumerate(((grad, g_ref), (gated, u_ref), (value, v_ref)))
    ]
    for load in loads:
        load.start()

    barrier = pltpu.get_barrier_semaphore()
    for r in range(SEQ - 1):
        pl.semaphore_signal(barrier, inc=1, device_id=(dp, ahead(r)), device_id_type=MESH)
    other_dp(
        lambda r: pl.semaphore_signal(
            barrier, inc=1, device_id=((dp + r) % DP, sq), device_id_type=MESH
        )
    )

    loads[0].wait()
    loads[1].wait()
    bias_acc[...] = jnp.zeros_like(bias_acc)

    def make_d(panel):
        at = lanes(panel * WIDTH, WIDTH)
        d = (g_ref[:, at].astype(F32) * u_ref[:, at].astype(F32)).astype(BF16)
        wide = d.astype(F32)
        bias_acc[...] += wide[:, :BLOCK] + wide[:, BLOCK:]
        return d

    my_rows = rows(sq * TOK, TOK)
    d_buf[ahead(0)] = make_d(ahead(0))
    pl.semaphore_wait(barrier, SEQ - 1 + DP - 1)
    for r in range(SEQ - 1):
        panel = ahead(r)
        if r > 0:
            d_buf[panel] = make_d(panel)
        to_seq(S_D, r, d_buf.at[panel], d_pad.at[my_rows]).start()
    d_pad[my_rows] = make_d(sq)

    loads[2].wait()

    def norm_rows(c, carry):
        at = rows(c * CHUNK, CHUNK)
        total = jnp.zeros((CHUNK, WIDTH), F32)
        for p in range(SEQ):
            total += v_ref[at, p * WIDTH : (p + 1) * WIDTH].astype(F32)
        mean = jnp.sum(total, axis=1, keepdims=True) * (1.0 / FEAT)
        total = jnp.zeros((CHUNK, WIDTH), F32)
        for p in range(SEQ):
            centered = v_ref[at, p * WIDTH : (p + 1) * WIDTH].astype(F32) - mean
            total += centered * centered
        inv = lax.rsqrt(jnp.sum(total, axis=1, keepdims=True) * (1.0 / FEAT) + EPS)
        inv_ref[at] = jnp.broadcast_to(inv, (CHUNK, BLOCK))
        for p in range(SEQ):
            cut = slice(p * WIDTH, (p + 1) * WIDTH)
            hat = (v_ref[at, cut].astype(F32) - mean) * inv
            hat_ref[at, cut] = hat
            n_buf[p, at] = (hat * gain[:, cut]).astype(BF16)
        return carry

    lax.fori_loop(0, TOK // CHUNK, norm_rows, 0)
    my_padded = rows(PAD + sq * TOK, TOK)
    for r in range(SEQ - 1):
        to_seq(S_N, r, n_buf.at[ahead(r)], n_pad.at[my_padded]).start()
    n_pad[my_padded] = n_buf[sq]

    part_bias = bias_acc[...].T.reshape(BLOCK // 8, 8, TOK)
    bias_all[dp] = jnp.sum(part_bias, axis=0)
    other_dp(lambda r: to_dp(S_BIAS, r, bias_all.at[dp], bias_all.at[dp]).start())

    zero_block = jnp.zeros((BLOCK, BLOCK), BF16)
    row_ids = lax.broadcasted_iota(jnp.int32, (BLOCK, BLOCK), 0)
    col_ids = lax.broadcasted_iota(jnp.int32, (BLOCK, BLOCK), 1)
    lower = row_ids >= col_ids
    for i, m in ((0, BAND), (1, 0)):
        for matrix in (band, band_t):
            matrix[i * BLOCK : (i + 1) * BLOCK, m * BLOCK : (m + 1) * BLOCK] = zero_block
    for k in range(SLOTS):
        w32 = weights[k].astype(F32)
        if k == 0:
            w32 = jnp.where(lower, w32, 0.0)
        w = w32.astype(BF16)
        wt32 = w32.T
        wt = wt32.astype(BF16)
        if k < BAND:
            for i in range(2):
                at = slice(i * BLOCK, (i + 1) * BLOCK)
                m = i + BAND - 1 - k
                band[at, m * BLOCK : (m + 1) * BLOCK] = w
                m = i + k
                band_t[at, m * BLOCK : (m + 1) * BLOCK] = wt
        else:
            wt_ref[k - BAND] = wt32

    far_rows = GROUPS * 2 - BAND

    def corner_row(j, carry):
        for i in range(far_rows):
            block = jnp.zeros((BLOCK, BLOCK), F32)
            for s in range(NSTR):
                hit = jnp.broadcast_to(cols[BAND + i : BAND + i + 1, s : s + 1], (BLOCK, BLOCK)) == j
                block += jnp.where(hit, wt_ref[s], 0.0)
            corner_t[rows(j * BLOCK, BLOCK), i * BLOCK : (i + 1) * BLOCK] = block.astype(BF16)
        return carry

    lax.fori_loop(0, far_rows, corner_row, 0)
    d_pad[TOTAL:] = jnp.zeros((PAD, WIDTH), BF16)
    n_pad[:PAD] = jnp.zeros((PAD, WIDTH), BF16)
    nt_pad[:, :PAD] = jnp.zeros((WIDTH, PAD), BF16)
    nt_pad[:, PAD + TOTAL :] = jnp.zeros((WIDTH, BLOCK), BF16)

    for r in range(SEQ - 1):
        from_seq(S_D, r, d_pad.at[rows(behind(r) * TOK, TOK)])

    def back_near(j, carry):
        out = jnp.dot(band_t[...], d_pad[rows(j * 256, SPAN)], preferred_element_type=F32)
        dn_all[rows(j * 256, 256)] = out.astype(BF16)
        return carry

    def back_far(j, carry):
        out = jnp.dot(band_t[...], d_pad[rows(j * 256, SPAN)], preferred_element_type=F32)
        out += jnp.dot(
            corner_t[rows(j * 256, 256)], d_pad[BAND * BLOCK : TOTAL], preferred_element_type=F32
        )
        dn_all[rows(j * 256, 256)] = out.astype(BF16)
        return carry

    lax.fori_loop(0, far_rows // 2, back_far, 0)
    lax.fori_loop(far_rows // 2, GROUPS, back_near, 0)
    for r in range(SEQ - 1):
        to_seq(S_DN, r, dn_all.at[rows(ahead(r) * TOK, TOK)], dn_back.at[sq]).start()
    dn_back[sq] = dn_all[my_rows]

    for r in range(SEQ - 1):
        from_seq(S_N, r, n_pad.at[rows(PAD + behind(r) * TOK, TOK)])

    g1_buf[...] = jnp.zeros_like(g1_buf)

    def turn(i, carry):
        block = n_pad[rows(PAD + i * 256, 256)]
        wide = block.astype(F32)
        nt_pad[:, lanes(PAD + i * 256, 256)] = block.T
        dn = dn_all[rows(i * 256, 256)].astype(F32)
        g1_buf[...] += jnp.sum((dn * wide).reshape(32, 8, WIDTH), axis=0)
        return carry

    lax.fori_loop(0, GROUPS, turn, 0)
    g1[dp] = g1_buf[...]
    other_dp(lambda r: to_dp(S_G1, r, g1_buf, g1.at[dp]).start())

    def slots(m, carry):
        acc = jnp.zeros((256, 256), F32)
        for i in range(GROUPS):
            acc += jnp.dot(
                d_pad[i * 256 : (i + 1) * 256],
                nt_pad[:, lanes(i * 256 + m * 256, 256)],
                preferred_element_type=F32,
            )
        sums[m] = acc
        return carry

    lax.fori_loop(0, (BAND + 2) // 2, slots, 0)
    for i in range(far_rows):
        for s in range(NSTR):
            col = jnp.broadcast_to(cols[BAND + i : BAND + i + 1, s : s + 1], (BLOCK, WIDTH))
            block = n_pad[PAD : PAD + BLOCK].astype(F32)
            for c in range(1, i + 1):
                other = n_pad[PAD + c * BLOCK : PAD + (c + 1) * BLOCK].astype(F32)
                block = jnp.where(col == c, other, block)
            picked[i, s * BLOCK : (s + 1) * BLOCK] = block.astype(BF16)
    far = jnp.zeros((BLOCK, 2 * BLOCK), F32)
    for i in range(far_rows):
        far += lax.dot_general(
            d_pad[(BAND + i) * BLOCK : (BAND + i + 1) * BLOCK],
            picked[i],
            (((1,), (1,)), ((), ())),
            preferred_element_type=F32,
        )
    for k in range(SLOTS):
        if k < BAND:
            m0, m1 = BAND - 1 - k, BAND - k
            grad_k = (
                sums[m0 // 2, :BLOCK, (m0 % 2) * BLOCK : (m0 % 2 + 1) * BLOCK]
                + sums[m1 // 2, BLOCK:, (m1 % 2) * BLOCK : (m1 % 2 + 1) * BLOCK]
            )
        else:
            grad_k = far[:, (k - BAND) * BLOCK : (k - BAND + 1) * BLOCK]
        if k == 0:
            grad_k = jnp.where(lower, grad_k, 0.0)
        slot_buf[k * BLOCK : (k + 1) * BLOCK] = grad_k.astype(BF16)
    other_dp(
        lambda r: to_dp(
            S_R1, r, slot_buf.at[rows(((dp + r) % DP) * PIECE, PIECE)], r1.at[dp]
        ).start()
    )
    r1[dp] = slot_buf[rows(dp * PIECE, PIECE)]

    bias_t = bias[...].T
    two = 2 * BLOCK
    far_w = jnp.concatenate([weights[BAND], weights[BAND + 1]], axis=1)
    for i in range(GROUPS):
        out = jnp.dot(band[...], n_pad[i * two : i * two + SPAN], preferred_element_type=F32)
        for h in range(2):
            half = out[h * BLOCK : (h + 1) * BLOCK]
            b = 2 * i + h
            if b >= BAND:
                half += jnp.dot(far_w, picked[b - BAND], preferred_element_type=F32)
            half += bias_t[:, b : b + 1]
            mx_all[b * BLOCK : (b + 1) * BLOCK] = half.astype(BF16)

    def send_mixed(r):
        to_seq(S_MX, r, mx_all.at[rows(ahead(r) * TOK, TOK)], mx_back.at[sq]).start()

    other_dp(lambda r: from_dp(S_G1, r, g1.at[(dp + DP - r) % DP]))
    total = jnp.sum(jnp.sum(g1[...], axis=0), axis=0, keepdims=True)
    my_gain = gain[:, lanes(sq * WIDTH, WIDTH)]
    g2[sq] = jnp.broadcast_to(total / (my_gain * math.sqrt(DP * TOTAL)), (8, WIDTH))
    for r in range(SEQ - 1):
        to_seq(S_G2, r, g2.at[sq], g2.at[sq]).start()

    other_dp(lambda r: from_dp(S_R1, r, r1.at[(dp + DP - r) % DP]))

    def sum_piece(t, carry):
        part[t] = jnp.sum(r1[:, rows(t * SUB, SUB), :].astype(F32), axis=0)
        return carry

    lax.fori_loop(0, REDUCERS, sum_piece, 0)
    for r in range(SEQ - 1):
        @pl.when(ahead(r) < REDUCERS)
        def _():
            to_seq(S_R2, r, part.at[ahead(r)], r2.at[sq]).start()

    for r in range(MIX_FIRST):
        send_mixed(r)

    @pl.when(sq < REDUCERS)
    def _():
        r2[sq] = part[sq]
        for r in range(SEQ - 1):
            from_seq(S_R2, r, r2.at[behind(r)])
        r2b[sq] = jnp.sum(r2[...], axis=0)
        for r in range(SEQ - 1):
            to_seq(S_R2B, r, r2b.at[sq], r2b.at[sq]).start()

    for r in range(MIX_FIRST, SEQ - 1):
        send_mixed(r)
    mx_back[sq] = mx_all[my_rows]

    for r in range(SEQ - 1):
        from_seq(S_DN, r, dn_back.at[behind(r)])

    def value_rows(c, carry):
        at = rows(c * CHUNK, CHUNK)
        first = jnp.zeros((CHUNK, WIDTH), F32)
        second = jnp.zeros((CHUNK, WIDTH), F32)
        for p in range(SEQ):
            cut = slice(p * WIDTH, (p + 1) * WIDTH)
            hat_grad = dn_back[p, at].astype(F32) * gain[:, cut]
            first += hat_grad
            second += hat_grad * hat_ref[at, cut]
        mean1 = jnp.sum(first, axis=1, keepdims=True) * (1.0 / FEAT)
        mean2 = jnp.sum(second, axis=1, keepdims=True) * (1.0 / FEAT)
        inv = inv_ref[at][:, :1]
        for p in range(SEQ):
            cut = slice(p * WIDTH, (p + 1) * WIDTH)
            hat_grad = dn_back[p, at].astype(F32) * gain[:, cut]
            out = inv * (hat_grad - mean1 - hat_ref[at, cut] * mean2)
            value_grad[at, cut] = out.astype(BF16)
        return carry

    lax.fori_loop(0, TOK // CHUNK, value_rows, 0)

    for r in range(SEQ - 1):
        @pl.when(behind(r) < REDUCERS)
        def _():
            from_seq(S_R2B, r, r2b.at[behind(r)])

    for t in range(REDUCERS):
        r3_buf[t * SUB : (t + 1) * SUB] = r2b[t].astype(BF16)
    other_dp(lambda r: to_dp(S_R3, r, r3_buf, r3.at[dp]).start())
    r3[dp] = r3_buf[...]

    other_dp(lambda r: from_dp(S_BIAS, r, bias_all.at[(dp + DP - r) % DP]))
    bias_sum = jnp.sum(jnp.sum(bias_all[...], axis=0), axis=0, keepdims=True)
    bias_grad[...] = bias_sum * (1.0 / math.sqrt(DP * FEAT))
    for r in range(SEQ - 1):
        from_seq(S_G2, r, g2.at[behind(r)])
    for p in range(SEQ):
        gain_grad[:, p * WIDTH : (p + 1) * WIDTH] = g2[p, :1]

    def finish(panel):
        at = lanes(panel * WIDTH, WIDTH)
        gated_grad[:, at] = (g_ref[:, at].astype(F32) * mx_back[panel].astype(F32)).astype(BF16)

    finish(sq)
    for r in range(SEQ - 1):
        from_seq(S_MX, r, mx_back.at[behind(r)])
        finish(behind(r))

    scale = 1.0 / math.sqrt(DP * TOTAL * FEAT)
    weight_grad[rows(dp * PIECE, PIECE)] = r3[dp].astype(F32) * scale

    def last(r):
        piece = (dp + DP - r) % DP
        from_dp(S_R3, r, r3.at[piece])
        weight_grad[rows(piece * PIECE, PIECE)] = r3[piece].astype(F32) * scale

    other_dp(last)

    for r in range(SEQ - 1):
        to_seq(S_D, r, d_buf.at[ahead(r)], d_pad.at[my_rows]).wait_send()
        to_seq(S_N, r, n_buf.at[ahead(r)], n_pad.at[my_padded]).wait_send()
        to_seq(S_DN, r, dn_all.at[rows(ahead(r) * TOK, TOK)], dn_back.at[sq]).wait_send()
        to_seq(S_MX, r, mx_all.at[rows(ahead(r) * TOK, TOK)], mx_back.at[sq]).wait_send()
        to_seq(S_G2, r, g2.at[sq], g2.at[sq]).wait_send()

        @pl.when(ahead(r) < REDUCERS)
        def _():
            to_seq(S_R2, r, part.at[ahead(r)], r2.at[sq]).wait_send()

        @pl.when(sq < REDUCERS)
        def _():
            to_seq(S_R2B, r, r2b.at[sq], r2b.at[sq]).wait_send()

    def sent(r):
        to_dp(S_BIAS, r, bias_all.at[dp], bias_all.at[dp]).wait_send()
        to_dp(S_G1, r, g1_buf, g1.at[dp]).wait_send()
        to_dp(
            S_R1, r, slot_buf.at[rows(((dp + r) % DP) * PIECE, PIECE)], r1.at[dp]
        ).wait_send()
        to_dp(S_R3, r, r3_buf, r3.at[dp]).wait_send()

    other_dp(sent)


def shards(gated_part, mixed_part, out_grad, norm_gain, mix_bias, token_mixing_weight, stride_cols):
    vmem = pl.BlockSpec(memory_space=pltpu.VMEM)
    hbm = pl.BlockSpec(memory_space=pl.ANY)
    wide = (TOK, FEAT)
    panels = (SEQ, TOK, WIDTH)
    scratch = [
        (wide, BF16), (wide, BF16), (wide, BF16), (wide, F32), ((TOK, BLOCK), F32),
        (panels, BF16), (panels, BF16),
        ((TOTAL + PAD, WIDTH), BF16), ((TOTAL + PAD, WIDTH), BF16),
        ((WIDTH, TOTAL + SPAN - BLOCK), BF16),
        ((TOTAL, WIDTH), BF16), ((TOTAL, WIDTH), BF16), (panels, BF16), (panels, BF16),
        ((2 * BLOCK, SPAN), BF16), ((2 * BLOCK, SPAN), BF16), ((8 * BLOCK, 8 * BLOCK), BF16),
        ((NSTR, BLOCK, BLOCK), F32), ((8, NSTR * BLOCK, WIDTH), BF16),
        (((BAND + 2) // 2, 256, 256), F32), ((SLOTS * BLOCK, BLOCK), BF16),
        ((DP, PIECE, BLOCK), BF16), ((REDUCERS, SUB, BLOCK), F32), ((SEQ, SUB, BLOCK), F32),
        ((REDUCERS, SUB, BLOCK), F32), ((PIECE, BLOCK), BF16), ((DP, PIECE, BLOCK), BF16),
        ((TOK, BLOCK), F32), ((DP, 8, TOK), F32),
        ((8, WIDTH), F32), ((DP, 8, WIDTH), F32), ((SEQ, 8, WIDTH), F32),
    ]
    outs = pl.pallas_call(
        kernel,
        out_shape=(
            jax.ShapeDtypeStruct(wide, BF16),
            jax.ShapeDtypeStruct(wide, BF16),
            jax.ShapeDtypeStruct((SLOTS * BLOCK, BLOCK), F32),
            jax.ShapeDtypeStruct((1, FEAT), F32),
            jax.ShapeDtypeStruct((1, TOK), F32),
        ),
        in_specs=[hbm, hbm, hbm, vmem, vmem, vmem, vmem],
        out_specs=[vmem] * 5,
        scratch_shapes=[pltpu.VMEM(shape, kind) for shape, kind in scratch]
        + [
            pltpu.SemaphoreType.DMA((3,)),
            pltpu.SemaphoreType.DMA((PHASES, SEQ)),
            pltpu.SemaphoreType.DMA((PHASES, SEQ)),
        ],
        compiler_params=pltpu.CompilerParams(
            collective_id=0, has_side_effects=True, vmem_limit_bytes=56 * 2**20
        ),
    )(
        gated_part[0],
        mixed_part[0],
        out_grad[0],
        norm_gain.reshape(1, FEAT),
        mix_bias.reshape(TOTAL // BLOCK, BLOCK),
        token_mixing_weight,
        stride_cols,
    )
    gated_grad, value_grad, weight_grad, gain_grad, bias_grad = outs
    return (
        gated_grad[None],
        value_grad[None],
        weight_grad.reshape(SLOTS, BLOCK, BLOCK),
        gain_grad.reshape(FEAT),
        bias_grad.reshape(TOK),
    )


def solution(mesh):
    placed = (P("dp", "seq", None), P("dp", "seq", None), P("dp", "seq", None), P(), P(), P(), P())
    return jax.shard_map(
        shards,
        mesh=mesh,
        in_specs=placed,
        out_specs=(P("dp", "seq", None), P("dp", "seq", None), P(), P(), P("seq")),
        check_vma=False,
    )
```

```python
import math

import jax
import jax.numpy as jnp
from jax import lax
from jax.experimental import pallas as pl
from jax.experimental.pallas import tpu as pltpu
from jax.sharding import PartitionSpec as P

BLOCK = 128
BAND = 16
NSTR = 2
EPS = 1e-05
MESH = pl.DeviceIdType.MESH
F32 = jnp.float32
BF16 = jnp.bfloat16

OFFSETS = (
    (2, 2), (1, 2), (2, 1), (3, 2), (2, 3), (1, 1), (3, 3), (1, 3),
    (3, 1), (0, 2), (2, 0), (0, 1), (1, 0), (0, 3), (3, 0),
)

SEQ = 16
DP = 16
TOK = 192
FEAT = 4096
WIDTH = FEAT // SEQ
TOTAL = TOK * SEQ
GROUPS = TOTAL // (2 * BLOCK)
SPAN = (BAND + 1) * BLOCK
PAD = (BAND - 1) * BLOCK
SUMS = (BAND + 2) * BLOCK
SLOTS = BAND + NSTR
PIECE = SLOTS * BLOCK // DP
SUB = 16
DEPTH = 8
HALF = DEPTH * PIECE
REDUCERS = PIECE // SUB
CHUNK = 16

S_D, S_N, S_DN, S_MX, S_R1, S_R2, S_R2B, S_R3, S_BIAS, S_G1, S_G2, S_R0, S_R4 = range(13)
PHASES = 13
BACK_FIRST = 6
MIX_FIRST = 3
MIX_SECOND = 7


def weave(first, second):
    order = []
    for i, item in enumerate(first):
        order.append((True, item))
        order += [(False, other) for q, other in enumerate(second) if q * len(first) // len(second) == i]
    return order


def rows(start, size):
    return pl.ds(pl.multiple_of(start, 16), size)


def lanes(start, size):
    return pl.ds(pl.multiple_of(start, 128), size)


def kernel(
    gated, value, grad, gain_in, bias_in, weights_in, cols_in,
    gated_grad, value_grad, weight_grad, gain_grad, bias_grad,
    u_ref, v_ref, g_ref, gain, bias, weights, cols, hat_ref, inv_ref,
    d_buf, n_buf, d_pad, n_pad, dn_all, mx_all, dn_back, mx_back,
    band, band_t, corner_t, wt_ref, picked, sums, slot_buf,
    r0, half_buf, r1, part, r2, r2b, r3_buf, r3, bias_acc, bias_all, g1_buf, g1, g2,
    in_sem, ss, rs,
):
    dp = lax.axis_index("dp")
    sq = lax.axis_index("seq")
    x, y = sq // 4, sq % 4
    z, core = dp // 2, dp % 2

    def ahead(r):
        dx, dy = OFFSETS[r]
        return ((x + dx) % 4) * 4 + (y + dy) % 4

    def behind(r):
        dx, dy = OFFSETS[r]
        return ((x + 4 - dx) % 4) * 4 + (y + 4 - dy) % 4

    def to_seq(phase, r, src, dst):
        return pltpu.make_async_remote_copy(
            src_ref=src, dst_ref=dst, send_sem=ss.at[phase, r], recv_sem=rs.at[phase, r],
            device_id=(dp, ahead(r)), device_id_type=MESH,
        )

    def from_seq(phase, r, slot):
        pltpu.make_async_remote_copy(
            src_ref=slot, dst_ref=slot, send_sem=ss.at[phase, r], recv_sem=rs.at[phase, r],
            device_id=(dp, behind(r)), device_id_type=MESH,
        ).wait_recv()

    def to_dp(phase, r, src, dst):
        return pltpu.make_async_remote_copy(
            src_ref=src, dst_ref=dst, send_sem=ss.at[phase, r], recv_sem=rs.at[phase, r],
            device_id=((dp + r) % DP, sq), device_id_type=MESH,
        )

    def from_dp(phase, r, slot):
        pltpu.make_async_remote_copy(
            src_ref=slot, dst_ref=slot, send_sem=ss.at[phase, r], recv_sem=rs.at[phase, r],
            device_id=((dp + DP - r) % DP, sq), device_id_type=MESH,
        ).wait_recv()

    def to_z(phase, r, src, dst):
        return pltpu.make_async_remote_copy(
            src_ref=src, dst_ref=dst, send_sem=ss.at[phase, r], recv_sem=rs.at[phase, r],
            device_id=(((z + r) % DEPTH) * 2 + core, sq), device_id_type=MESH,
        )

    def from_z(phase, r, slot):
        pltpu.make_async_remote_copy(
            src_ref=slot, dst_ref=slot, send_sem=ss.at[phase, r], recv_sem=rs.at[phase, r],
            device_id=(((z + DEPTH - r) % DEPTH) * 2 + core, sq), device_id_type=MESH,
        ).wait_recv()

    def to_core(phase, src, dst):
        return pltpu.make_async_remote_copy(
            src_ref=src, dst_ref=dst, send_sem=ss.at[phase, 0], recv_sem=rs.at[phase, 0],
            device_id=(z * 2 + 1 - core, sq), device_id_type=MESH,
        )

    def other_dp(body):
        def step(r, carry):
            body(r)
            return carry

        lax.fori_loop(1, DP, step, 0)

    loads = [
        pltpu.make_async_copy(src, dst, in_sem.at[i])
        for i, (src, dst) in enumerate(
            (
                (grad, g_ref), (gated, u_ref), (value, v_ref), (gain_in, gain),
                (bias_in, bias), (weights_in, weights), (cols_in, cols),
            )
        )
    ]
    for load in loads:
        load.start()

    barrier = pltpu.get_barrier_semaphore()
    for r in range(SEQ - 1):
        pl.semaphore_signal(barrier, inc=1, device_id=(dp, ahead(r)), device_id_type=MESH)
    other_dp(
        lambda r: pl.semaphore_signal(
            barrier, inc=1, device_id=((dp + r) % DP, sq), device_id_type=MESH
        )
    )

    loads[0].wait()
    loads[1].wait()
    bias_acc[...] = jnp.zeros_like(bias_acc)

    def make_d(panel):
        at = lanes(panel * WIDTH, WIDTH)
        d = (g_ref[:, at].astype(F32) * u_ref[:, at].astype(F32)).astype(BF16)
        wide = d.astype(F32)
        bias_acc[...] += wide[:, :BLOCK] + wide[:, BLOCK:]
        return d

    my_rows = rows(sq * TOK, TOK)
    d_buf[ahead(0)] = make_d(ahead(0))
    pl.semaphore_wait(barrier, SEQ - 1 + DP - 1)
    for r in range(SEQ - 1):
        panel = ahead(r)
        if r > 0:
            d_buf[panel] = make_d(panel)
        to_seq(S_D, r, d_buf.at[panel], d_pad.at[my_rows]).start()
    d_pad[my_rows] = make_d(sq)

    for load in loads[2:]:
        load.wait()

    def norm_rows(c, carry):
        at = rows(c * CHUNK, CHUNK)
        total = jnp.zeros((CHUNK, WIDTH), F32)
        for p in range(SEQ):
            total += v_ref[at, p * WIDTH : (p + 1) * WIDTH].astype(F32)
        mean = jnp.sum(total, axis=1, keepdims=True) * (1.0 / FEAT)
        total = jnp.zeros((CHUNK, WIDTH), F32)
        for p in range(SEQ):
            centered = v_ref[at, p * WIDTH : (p + 1) * WIDTH].astype(F32) - mean
            total += centered * centered
        inv = lax.rsqrt(jnp.sum(total, axis=1, keepdims=True) * (1.0 / FEAT) + EPS)
        inv_ref[at] = jnp.broadcast_to(inv, (CHUNK, BLOCK))
        for p in range(SEQ):
            cut = slice(p * WIDTH, (p + 1) * WIDTH)
            hat = (v_ref[at, cut].astype(F32) - mean) * inv
            hat_ref[at, cut] = hat
            n_buf[p, at] = (hat * gain[:, cut]).astype(BF16)
        return carry

    lax.fori_loop(0, TOK // CHUNK, norm_rows, 0)
    my_padded = rows(PAD + sq * TOK, TOK)
    for r in range(SEQ - 1):
        to_seq(S_N, r, n_buf.at[ahead(r)], n_pad.at[my_padded]).start()
    n_pad[my_padded] = n_buf[sq]

    part_bias = bias_acc[...].T.reshape(BLOCK // 8, 8, TOK)
    bias_all[dp] = jnp.sum(part_bias, axis=0)
    other_dp(lambda r: to_dp(S_BIAS, r, bias_all.at[dp], bias_all.at[dp]).start())

    zero_block = jnp.zeros((BLOCK, BLOCK), BF16)
    row_ids = lax.broadcasted_iota(jnp.int32, (BLOCK, BLOCK), 0)
    col_ids = lax.broadcasted_iota(jnp.int32, (BLOCK, BLOCK), 1)
    lower = row_ids >= col_ids
    for i, m in ((0, BAND), (1, 0)):
        for matrix in (band, band_t):
            matrix[i * BLOCK : (i + 1) * BLOCK, m * BLOCK : (m + 1) * BLOCK] = zero_block
    for k in range(SLOTS):
        w32 = weights[k].astype(F32)
        if k == 0:
            w32 = jnp.where(lower, w32, 0.0)
        w = w32.astype(BF16)
        wt32 = w32.T
        wt = wt32.astype(BF16)
        if k < BAND:
            for i in range(2):
                at = slice(i * BLOCK, (i + 1) * BLOCK)
                m = i + BAND - 1 - k
                band[at, m * BLOCK : (m + 1) * BLOCK] = w
                m = i + k
                band_t[at, m * BLOCK : (m + 1) * BLOCK] = wt
        else:
            wt_ref[k - BAND] = wt32

    far_rows = GROUPS * 2 - BAND

    def corner_row(j, carry):
        for i in range(far_rows):
            block = jnp.zeros((BLOCK, BLOCK), F32)
            for s in range(NSTR):
                hit = jnp.broadcast_to(cols[s : s + 1, BAND + i : BAND + i + 1], (BLOCK, BLOCK)) == j
                block += jnp.where(hit, wt_ref[s], 0.0)
            corner_t[rows(j * BLOCK, BLOCK), i * BLOCK : (i + 1) * BLOCK] = block.astype(BF16)
        return carry

    lax.fori_loop(0, far_rows, corner_row, 0)
    d_pad[TOTAL:] = jnp.zeros((PAD + BLOCK, WIDTH), BF16)
    n_pad[:PAD] = jnp.zeros((PAD, WIDTH), BF16)

    for r in range(SEQ - 1):
        from_seq(S_D, r, d_pad.at[rows(behind(r) * TOK, TOK)])

    def back_near(j, carry):
        out = jnp.dot(band_t[...], d_pad[rows(j * 256, SPAN)], preferred_element_type=F32)
        dn_all[rows(j * 256, 256)] = out.astype(BF16)
        return carry

    def back_far(j, carry):
        out = jnp.dot(band_t[...], d_pad[rows(j * 256, SPAN)], preferred_element_type=F32)
        out += jnp.dot(
            corner_t[rows(j * 256, 256)], d_pad[BAND * BLOCK : TOTAL], preferred_element_type=F32
        )
        dn_all[rows(j * 256, 256)] = out.astype(BF16)
        return carry

    lax.fori_loop(0, far_rows // 2, back_far, 0)
    lax.fori_loop(far_rows // 2, GROUPS, back_near, 0)

    def send_back(r):
        to_seq(S_DN, r, dn_all.at[rows(ahead(r) * TOK, TOK)], dn_back.at[sq]).start()

    for r in range(BACK_FIRST):
        send_back(r)
    dn_back[sq] = dn_all[my_rows]

    for r in range(SEQ - 1):
        from_seq(S_N, r, n_pad.at[rows(PAD + behind(r) * TOK, TOK)])

    g1_buf[...] = jnp.zeros_like(g1_buf)

    def turn(i, carry):
        wide = n_pad[rows(PAD + i * 256, 256)].astype(F32)
        dn = dn_all[rows(i * 256, 256)].astype(F32)
        g1_buf[...] += jnp.sum((dn * wide).reshape(32, 8, WIDTH), axis=0)
        return carry

    lax.fori_loop(0, GROUPS, turn, 0)
    g1[dp] = g1_buf[...]
    other_dp(lambda r: to_dp(S_G1, r, g1_buf, g1.at[dp]).start())

    sums[...] = jnp.zeros_like(sums)

    def slots(j, carry):
        sums[...] += lax.dot_general(
            d_pad[rows(j * 256, SUMS)],
            n_pad[rows(PAD + j * 256, 256)],
            (((1,), (1,)), ((), ())),
            preferred_element_type=F32,
        )
        return carry

    lax.fori_loop(0, GROUPS, slots, 0)
    for i in range(far_rows):
        for s in range(NSTR):
            col = jnp.broadcast_to(cols[s : s + 1, BAND + i : BAND + i + 1], (BLOCK, WIDTH))
            block = n_pad[PAD : PAD + BLOCK].astype(F32)
            for c in range(1, i + 1):
                other = n_pad[PAD + c * BLOCK : PAD + (c + 1) * BLOCK].astype(F32)
                block = jnp.where(col == c, other, block)
            picked[i, s * BLOCK : (s + 1) * BLOCK] = block.astype(BF16)
    far = jnp.zeros((BLOCK, 2 * BLOCK), F32)
    for i in range(far_rows):
        far += lax.dot_general(
            d_pad[(BAND + i) * BLOCK : (BAND + i + 1) * BLOCK],
            picked[i],
            (((1,), (1,)), ((), ())),
            preferred_element_type=F32,
        )
    for k in range(SLOTS):
        if k < BAND:
            grad_k = (
                sums[k * BLOCK : (k + 1) * BLOCK, :BLOCK]
                + sums[(k + 1) * BLOCK : (k + 2) * BLOCK, BLOCK:]
            )
        else:
            grad_k = far[:, (k - BAND) * BLOCK : (k - BAND + 1) * BLOCK]
        if k == 0:
            grad_k = jnp.where(lower, grad_k, 0.0)
        slot_buf[k * BLOCK : (k + 1) * BLOCK] = grad_k.astype(BF16)
    mine, theirs = rows(core * HALF, HALF), rows((1 - core) * HALF, HALF)
    swap = to_core(S_R0, slot_buf.at[theirs], r0)
    swap.start()
    swap.wait_recv()
    half_buf[...] = (slot_buf[mine].astype(F32) + r0[...].astype(F32)).astype(BF16)

    def z_rows(r):
        return rows(((z + r) % DEPTH) * PIECE, PIECE)

    for summed, r in weave(range(1, DEPTH), range(BACK_FIRST, SEQ - 1)):
        if summed:
            to_z(S_R1, r, half_buf.at[z_rows(r)], r1.at[z]).start()
        else:
            send_back(r)
    r1[z] = half_buf[z_rows(0)]

    bias_t = bias[...].T
    two = 2 * BLOCK
    far_w = jnp.concatenate([weights[BAND], weights[BAND + 1]], axis=1)
    for i in range(GROUPS):
        out = jnp.dot(band[...], n_pad[i * two : i * two + SPAN], preferred_element_type=F32)
        for h in range(2):
            half = out[h * BLOCK : (h + 1) * BLOCK]
            b = 2 * i + h
            if b >= BAND:
                half += jnp.dot(far_w, picked[b - BAND], preferred_element_type=F32)
            half += bias_t[:, b : b + 1]
            mx_all[b * BLOCK : (b + 1) * BLOCK] = half.astype(BF16)

    def send_mixed(r):
        to_seq(S_MX, r, mx_all.at[rows(ahead(r) * TOK, TOK)], mx_back.at[sq]).start()

    other_dp(lambda r: from_dp(S_G1, r, g1.at[(dp + DP - r) % DP]))
    total = jnp.sum(jnp.sum(g1[...], axis=0), axis=0, keepdims=True)
    my_gain = gain[:, lanes(sq * WIDTH, WIDTH)]
    g2[sq] = jnp.broadcast_to(total / (my_gain * math.sqrt(DP * TOTAL)), (8, WIDTH))
    for r in range(SEQ - 1):
        to_seq(S_G2, r, g2.at[sq], g2.at[sq]).start()

    for r in range(1, DEPTH):
        from_z(S_R1, r, r1.at[(z + DEPTH - r) % DEPTH])

    def sum_piece(t, carry):
        part[t] = jnp.sum(r1[:, rows(t * SUB, SUB), :].astype(F32), axis=0)
        return carry

    lax.fori_loop(0, REDUCERS, sum_piece, 0)
    for r in range(SEQ - 1):
        @pl.when(ahead(r) < REDUCERS)
        def _():
            to_seq(S_R2, r, part.at[ahead(r)], r2.at[sq]).start()

    for r in range(MIX_FIRST):
        send_mixed(r)

    @pl.when(sq < REDUCERS)
    def _():
        r2[sq] = part[sq]
        for r in range(SEQ - 1):
            from_seq(S_R2, r, r2.at[behind(r)])
        r2b[sq] = jnp.sum(r2[...], axis=0)
        for r in range(SEQ - 1):
            to_seq(S_R2B, r, r2b.at[sq], r2b.at[sq]).start()

    for r in range(MIX_FIRST, MIX_SECOND):
        send_mixed(r)
    mx_back[sq] = mx_all[my_rows]

    for r in range(SEQ - 1):
        @pl.when(behind(r) < REDUCERS)
        def _():
            from_seq(S_R2B, r, r2b.at[behind(r)])

    for t in range(REDUCERS):
        r3_buf[t * SUB : (t + 1) * SUB] = r2b[t].astype(BF16)
    my_piece = core * DEPTH + z
    for summed, r in weave(range(1, DEPTH), range(MIX_SECOND, SEQ - 1)):
        if summed:
            to_z(S_R3, r, r3_buf, r3.at[my_piece]).start()
        else:
            send_mixed(r)
    r3[my_piece] = r3_buf[...]

    for r in range(SEQ - 1):
        from_seq(S_DN, r, dn_back.at[behind(r)])

    def value_rows(c, carry):
        at = rows(c * CHUNK, CHUNK)
        first = jnp.zeros((CHUNK, WIDTH), F32)
        second = jnp.zeros((CHUNK, WIDTH), F32)
        for p in range(SEQ):
            cut = slice(p * WIDTH, (p + 1) * WIDTH)
            hat_grad = dn_back[p, at].astype(F32) * gain[:, cut]
            first += hat_grad
            second += hat_grad * hat_ref[at, cut]
        mean1 = jnp.sum(first, axis=1, keepdims=True) * (1.0 / FEAT)
        mean2 = jnp.sum(second, axis=1, keepdims=True) * (1.0 / FEAT)
        inv = inv_ref[at][:, :1]
        for p in range(SEQ):
            cut = slice(p * WIDTH, (p + 1) * WIDTH)
            hat_grad = dn_back[p, at].astype(F32) * gain[:, cut]
            out = inv * (hat_grad - mean1 - hat_ref[at, cut] * mean2)
            value_grad[at, cut] = out.astype(BF16)
        return carry

    lax.fori_loop(0, TOK // CHUNK, value_rows, 0)

    other_dp(lambda r: from_dp(S_BIAS, r, bias_all.at[(dp + DP - r) % DP]))
    bias_sum = jnp.sum(jnp.sum(bias_all[...], axis=0), axis=0, keepdims=True)
    bias_grad[...] = bias_sum * (1.0 / math.sqrt(DP * FEAT))
    for r in range(SEQ - 1):
        from_seq(S_G2, r, g2.at[behind(r)])
    for p in range(SEQ):
        gain_grad[:, p * WIDTH : (p + 1) * WIDTH] = g2[p, :1]

    def finish(panel):
        at = lanes(panel * WIDTH, WIDTH)
        gated_grad[:, at] = (g_ref[:, at].astype(F32) * mx_back[panel].astype(F32)).astype(BF16)

    finish(sq)
    for r in range(7):
        from_seq(S_MX, r, mx_back.at[behind(r)])
        finish(behind(r))

    for r in range(1, DEPTH):
        from_z(S_R3, r, r3.at[core * DEPTH + (z + DEPTH - r) % DEPTH])
    half = r3.at[pl.ds(core * DEPTH, DEPTH)]
    pass_on = to_core(S_R4, half, half)
    pass_on.start()
    scale = 1.0 / math.sqrt(DP * TOTAL * FEAT)

    def scale_half(which):
        for t in range(DEPTH):
            piece = which * DEPTH + t
            weight_grad[rows(piece * PIECE, PIECE)] = r3[piece].astype(F32) * scale

    scale_half(core)
    for r in range(7, SEQ - 1):
        from_seq(S_MX, r, mx_back.at[behind(r)])
        finish(behind(r))
    other = r3.at[pl.ds((1 - core) * DEPTH, DEPTH)]
    to_core(S_R4, other, other).wait_recv()
    scale_half(1 - core)

    for r in range(SEQ - 1):
        to_seq(S_D, r, d_buf.at[ahead(r)], d_pad.at[my_rows]).wait_send()
        to_seq(S_N, r, n_buf.at[ahead(r)], n_pad.at[my_padded]).wait_send()
        to_seq(S_DN, r, dn_all.at[rows(ahead(r) * TOK, TOK)], dn_back.at[sq]).wait_send()
        to_seq(S_MX, r, mx_all.at[rows(ahead(r) * TOK, TOK)], mx_back.at[sq]).wait_send()
        to_seq(S_G2, r, g2.at[sq], g2.at[sq]).wait_send()

        @pl.when(ahead(r) < REDUCERS)
        def _():
            to_seq(S_R2, r, part.at[ahead(r)], r2.at[sq]).wait_send()

        @pl.when(sq < REDUCERS)
        def _():
            to_seq(S_R2B, r, r2b.at[sq], r2b.at[sq]).wait_send()

    def sent(r):
        to_dp(S_BIAS, r, bias_all.at[dp], bias_all.at[dp]).wait_send()
        to_dp(S_G1, r, g1_buf, g1.at[dp]).wait_send()
    other_dp(sent)
    swap.wait_send()
    pass_on.wait_send()
    for r in range(1, DEPTH):
        to_z(S_R1, r, half_buf.at[z_rows(r)], r1.at[z]).wait_send()
        to_z(S_R3, r, r3_buf, r3.at[my_piece]).wait_send()


def shards(gated_part, mixed_part, out_grad, norm_gain, mix_bias, token_mixing_weight, stride_cols):
    vmem = pl.BlockSpec(memory_space=pltpu.VMEM)
    hbm = pl.BlockSpec(memory_space=pltpu.HBM)
    wide = (TOK, FEAT)
    panels = (SEQ, TOK, WIDTH)
    scratch = [
        (wide, BF16), (wide, BF16), (wide, BF16), ((1, FEAT), F32), ((TOTAL // BLOCK, BLOCK), F32),
        ((SLOTS, BLOCK, BLOCK), BF16), ((NSTR, TOTAL // BLOCK), jnp.int32), (wide, F32), ((TOK, BLOCK), F32),
        (panels, BF16), (panels, BF16),
        ((TOTAL + PAD + BLOCK, WIDTH), BF16), ((TOTAL + PAD, WIDTH), BF16),
        ((TOTAL, WIDTH), BF16), ((TOTAL, WIDTH), BF16), (panels, BF16), (panels, BF16),
        ((2 * BLOCK, SPAN), BF16), ((2 * BLOCK, SPAN), BF16), ((8 * BLOCK, 8 * BLOCK), BF16),
        ((NSTR, BLOCK, BLOCK), F32), ((8, NSTR * BLOCK, WIDTH), BF16),
        ((SUMS, 256), F32), ((SLOTS * BLOCK, BLOCK), BF16),
        ((HALF, BLOCK), BF16), ((HALF, BLOCK), BF16),
        ((DEPTH, PIECE, BLOCK), BF16), ((REDUCERS, SUB, BLOCK), F32), ((SEQ, SUB, BLOCK), F32),
        ((REDUCERS, SUB, BLOCK), F32), ((PIECE, BLOCK), BF16), ((DP, PIECE, BLOCK), BF16),
        ((TOK, BLOCK), F32), ((DP, 8, TOK), F32),
        ((8, WIDTH), F32), ((DP, 8, WIDTH), F32), ((SEQ, 8, WIDTH), F32),
    ]
    outs = pl.pallas_call(
        kernel,
        out_shape=(
            jax.ShapeDtypeStruct(wide, BF16),
            jax.ShapeDtypeStruct(wide, BF16),
            jax.ShapeDtypeStruct((SLOTS * BLOCK, BLOCK), F32),
            jax.ShapeDtypeStruct((1, FEAT), F32),
            jax.ShapeDtypeStruct((1, TOK), F32),
        ),
        in_specs=[hbm] * 7,
        out_specs=[vmem] * 5,
        scratch_shapes=[pltpu.VMEM(shape, kind) for shape, kind in scratch]
        + [
            pltpu.SemaphoreType.DMA((7,)),
            pltpu.SemaphoreType.DMA((PHASES, SEQ)),
            pltpu.SemaphoreType.DMA((PHASES, SEQ)),
        ],
        compiler_params=pltpu.CompilerParams(
            collective_id=0, has_side_effects=True, vmem_limit_bytes=56 * 2**20
        ),
    )(
        gated_part[0],
        mixed_part[0],
        out_grad[0],
        norm_gain.reshape(1, FEAT),
        mix_bias.reshape(TOTAL // BLOCK, BLOCK),
        token_mixing_weight,
        stride_cols.T,
    )
    gated_grad, value_grad, weight_grad, gain_grad, bias_grad = outs
    return (
        gated_grad[None],
        value_grad[None],
        weight_grad.reshape(SLOTS, BLOCK, BLOCK),
        gain_grad.reshape(FEAT),
        bias_grad.reshape(TOK),
    )


def solution(mesh):
    placed = (P("dp", "seq", None), P("dp", "seq", None), P("dp", "seq", None), P(), P(), P(), P())
    return jax.shard_map(
        shards,
        mesh=mesh,
        in_specs=placed,
        out_specs=(P("dp", "seq", None), P("dp", "seq", None), P(), P(), P("seq")),
        check_vma=False,
    )
```

```python
import math

import jax
import jax.numpy as jnp
from jax import lax
from jax.experimental import pallas as pl
from jax.experimental.pallas import tpu as pltpu
from jax.sharding import PartitionSpec as P

BLOCK = 128
BAND = 16
NSTR = 2
EPS = 1e-05
MESH = pl.DeviceIdType.MESH
F32 = jnp.float32
BF16 = jnp.bfloat16

OFFSETS = (
    (2, 2), (1, 2), (2, 1), (3, 2), (2, 3), (1, 1), (3, 3), (1, 3),
    (3, 1), (0, 2), (2, 0), (0, 1), (1, 0), (0, 3), (3, 0),
)

SEQ = 16
DP = 16
TOK = 192
FEAT = 4096
WIDTH = FEAT // SEQ
TOTAL = TOK * SEQ
GROUPS = TOTAL // (2 * BLOCK)
SPAN = (BAND + 1) * BLOCK
PAD = (BAND - 1) * BLOCK
SUMS = (BAND + 2) * BLOCK
SLOTS = BAND + NSTR
PIECE = SLOTS * BLOCK // DP
SUB = 16
DEPTH = 8
HALF = DEPTH * PIECE
REDUCERS = PIECE // SUB
CHUNK = 16

S_D, S_N, S_DN, S_MX, S_R1, S_R2, S_R2B, S_R3, S_BIAS, S_G1, S_G2, S_R0, S_R4 = range(13)
PHASES = 13
BACK_FIRST = 9
MIX_FIRST = 1
MIX_SECOND = 4


def weave(first, second):
    order = []
    for i, item in enumerate(first):
        order.append((True, item))
        order += [(False, other) for q, other in enumerate(second) if q * len(first) // len(second) == i]
    return order


def rows(start, size):
    return pl.ds(pl.multiple_of(start, 16), size)


def lanes(start, size):
    return pl.ds(pl.multiple_of(start, 128), size)


def kernel(
    gated, value, grad, gain_in, bias_in, weights_in, cols_in,
    gated_grad, value_grad, weight_grad, gain_grad, bias_grad,
    u_ref, v_ref, g_ref, gain, bias, weights, cols, hat_ref, inv_ref,
    d_buf, n_buf, d_pad, n_pad, dn_all, mx_all, dn_back, mx_back,
    band, band_t, corner_t, wt_ref, picked, sums, slot_buf,
    r0, half_buf, r1, part, r2, r2b, r3_buf, r3, bias_acc, bias_all, g1_buf, g1, g2,
    in_sem, ss, rs,
):
    dp = lax.axis_index("dp")
    sq = lax.axis_index("seq")
    x, y = sq // 4, sq % 4
    z, core = dp // 2, dp % 2

    def ahead(r):
        dx, dy = OFFSETS[r]
        return ((x + dx) % 4) * 4 + (y + dy) % 4

    def behind(r):
        dx, dy = OFFSETS[r]
        return ((x + 4 - dx) % 4) * 4 + (y + 4 - dy) % 4

    def to_seq(phase, r, src, dst):
        return pltpu.make_async_remote_copy(
            src_ref=src, dst_ref=dst, send_sem=ss.at[phase, r], recv_sem=rs.at[phase, r],
            device_id=(dp, ahead(r)), device_id_type=MESH,
        )

    def from_seq(phase, r, slot):
        pltpu.make_async_remote_copy(
            src_ref=slot, dst_ref=slot, send_sem=ss.at[phase, r], recv_sem=rs.at[phase, r],
            device_id=(dp, behind(r)), device_id_type=MESH,
        ).wait_recv()

    def to_dp(phase, r, src, dst):
        return pltpu.make_async_remote_copy(
            src_ref=src, dst_ref=dst, send_sem=ss.at[phase, r], recv_sem=rs.at[phase, r],
            device_id=((dp + r) % DP, sq), device_id_type=MESH,
        )

    def from_dp(phase, r, slot):
        pltpu.make_async_remote_copy(
            src_ref=slot, dst_ref=slot, send_sem=ss.at[phase, r], recv_sem=rs.at[phase, r],
            device_id=((dp + DP - r) % DP, sq), device_id_type=MESH,
        ).wait_recv()

    def to_z(phase, r, src, dst):
        return pltpu.make_async_remote_copy(
            src_ref=src, dst_ref=dst, send_sem=ss.at[phase, r], recv_sem=rs.at[phase, r],
            device_id=(((z + r) % DEPTH) * 2 + core, sq), device_id_type=MESH,
        )

    def from_z(phase, r, slot):
        pltpu.make_async_remote_copy(
            src_ref=slot, dst_ref=slot, send_sem=ss.at[phase, r], recv_sem=rs.at[phase, r],
            device_id=(((z + DEPTH - r) % DEPTH) * 2 + core, sq), device_id_type=MESH,
        ).wait_recv()

    def to_core(phase, src, dst):
        return pltpu.make_async_remote_copy(
            src_ref=src, dst_ref=dst, send_sem=ss.at[phase, 0], recv_sem=rs.at[phase, 0],
            device_id=(z * 2 + 1 - core, sq), device_id_type=MESH,
        )

    def other_dp(body):
        def step(r, carry):
            body(r)
            return carry

        lax.fori_loop(1, DP, step, 0)

    loads = [
        pltpu.make_async_copy(src, dst, in_sem.at[i])
        for i, (src, dst) in enumerate(
            (
                (grad, g_ref), (gated, u_ref), (value, v_ref), (gain_in, gain),
                (bias_in, bias), (weights_in, weights), (cols_in, cols),
            )
        )
    ]
    for load in loads:
        load.start()

    barrier = pltpu.get_barrier_semaphore()
    for r in range(SEQ - 1):
        pl.semaphore_signal(barrier, inc=1, device_id=(dp, ahead(r)), device_id_type=MESH)
    other_dp(
        lambda r: pl.semaphore_signal(
            barrier, inc=1, device_id=((dp + r) % DP, sq), device_id_type=MESH
        )
    )

    loads[0].wait()
    loads[1].wait()
    bias_acc[...] = jnp.zeros_like(bias_acc)

    def make_d(panel):
        at = lanes(panel * WIDTH, WIDTH)
        d = (g_ref[:, at].astype(F32) * u_ref[:, at].astype(F32)).astype(BF16)
        wide = d.astype(F32)
        bias_acc[...] += wide[:, :BLOCK] + wide[:, BLOCK:]
        return d

    my_rows = rows(sq * TOK, TOK)
    d_buf[ahead(0)] = make_d(ahead(0))
    pl.semaphore_wait(barrier, SEQ - 1 + DP - 1)
    for r in range(SEQ - 1):
        panel = ahead(r)
        if r > 0:
            d_buf[panel] = make_d(panel)
        to_seq(S_D, r, d_buf.at[panel], d_pad.at[my_rows]).start()
    d_pad[my_rows] = make_d(sq)

    for load in loads[2:]:
        load.wait()

    def norm_rows(c, carry):
        at = rows(c * CHUNK, CHUNK)
        total = jnp.zeros((CHUNK, WIDTH), F32)
        for p in range(SEQ):
            total += v_ref[at, p * WIDTH : (p + 1) * WIDTH].astype(F32)
        mean = jnp.sum(total, axis=1, keepdims=True) * (1.0 / FEAT)
        total = jnp.zeros((CHUNK, WIDTH), F32)
        for p in range(SEQ):
            centered = v_ref[at, p * WIDTH : (p + 1) * WIDTH].astype(F32) - mean
            total += centered * centered
        inv = lax.rsqrt(jnp.sum(total, axis=1, keepdims=True) * (1.0 / FEAT) + EPS)
        inv_ref[at] = jnp.broadcast_to(inv, (CHUNK, BLOCK))
        for p in range(SEQ):
            cut = slice(p * WIDTH, (p + 1) * WIDTH)
            hat = (v_ref[at, cut].astype(F32) - mean) * inv
            hat_ref[at, cut] = hat
            n_buf[p, at] = (hat * gain[:, cut]).astype(BF16)
        return carry

    lax.fori_loop(0, TOK // CHUNK, norm_rows, 0)
    my_padded = rows(PAD + sq * TOK, TOK)
    for r in range(SEQ - 1):
        to_seq(S_N, r, n_buf.at[ahead(r)], n_pad.at[my_padded]).start()
    n_pad[my_padded] = n_buf[sq]

    part_bias = bias_acc[...].T.reshape(BLOCK // 8, 8, TOK)
    bias_all[dp] = jnp.sum(part_bias, axis=0)
    other_dp(lambda r: to_dp(S_BIAS, r, bias_all.at[dp], bias_all.at[dp]).start())

    zero_block = jnp.zeros((BLOCK, BLOCK), BF16)
    row_ids = lax.broadcasted_iota(jnp.int32, (BLOCK, BLOCK), 0)
    col_ids = lax.broadcasted_iota(jnp.int32, (BLOCK, BLOCK), 1)
    lower = row_ids >= col_ids
    for i, m in ((0, BAND), (1, 0)):
        for matrix in (band, band_t):
            matrix[i * BLOCK : (i + 1) * BLOCK, m * BLOCK : (m + 1) * BLOCK] = zero_block
    for k in range(SLOTS):
        w32 = weights[k].astype(F32)
        if k == 0:
            w32 = jnp.where(lower, w32, 0.0)
        w = w32.astype(BF16)
        wt32 = w32.T
        wt = wt32.astype(BF16)
        if k < BAND:
            for i in range(2):
                at = slice(i * BLOCK, (i + 1) * BLOCK)
                m = i + BAND - 1 - k
                band[at, m * BLOCK : (m + 1) * BLOCK] = w
                m = i + k
                band_t[at, m * BLOCK : (m + 1) * BLOCK] = wt
        else:
            wt_ref[k - BAND] = wt32

    far_rows = GROUPS * 2 - BAND

    def corner_row(j, carry):
        for i in range(far_rows):
            block = jnp.zeros((BLOCK, BLOCK), F32)
            for s in range(NSTR):
                hit = jnp.broadcast_to(cols[s : s + 1, BAND + i : BAND + i + 1], (BLOCK, BLOCK)) == j
                block += jnp.where(hit, wt_ref[s], 0.0)
            corner_t[rows(j * BLOCK, BLOCK), i * BLOCK : (i + 1) * BLOCK] = block.astype(BF16)
        return carry

    lax.fori_loop(0, far_rows, corner_row, 0)
    d_pad[TOTAL:] = jnp.zeros((PAD + BLOCK, WIDTH), BF16)
    n_pad[:PAD] = jnp.zeros((PAD, WIDTH), BF16)

    for r in range(SEQ - 1):
        from_seq(S_D, r, d_pad.at[rows(behind(r) * TOK, TOK)])

    def back_near(j, carry):
        out = jnp.dot(band_t[...], d_pad[rows(j * 256, SPAN)], preferred_element_type=F32)
        dn_all[rows(j * 256, 256)] = out.astype(BF16)
        return carry

    def back_far(j, carry):
        out = jnp.dot(band_t[...], d_pad[rows(j * 256, SPAN)], preferred_element_type=F32)
        out += jnp.dot(
            corner_t[rows(j * 256, 256)], d_pad[BAND * BLOCK : TOTAL], preferred_element_type=F32
        )
        dn_all[rows(j * 256, 256)] = out.astype(BF16)
        return carry

    lax.fori_loop(0, far_rows // 2, back_far, 0)
    lax.fori_loop(far_rows // 2, GROUPS, back_near, 0)

    def send_back(r):
        to_seq(S_DN, r, dn_all.at[rows(ahead(r) * TOK, TOK)], dn_back.at[sq]).start()

    for r in range(BACK_FIRST):
        send_back(r)
    dn_back[sq] = dn_all[my_rows]

    for r in range(SEQ - 1):
        from_seq(S_N, r, n_pad.at[rows(PAD + behind(r) * TOK, TOK)])

    g1_buf[...] = jnp.zeros_like(g1_buf)

    def turn(i, carry):
        wide = n_pad[rows(PAD + i * 256, 256)].astype(F32)
        dn = dn_all[rows(i * 256, 256)].astype(F32)
        g1_buf[...] += jnp.sum((dn * wide).reshape(32, 8, WIDTH), axis=0)
        return carry

    lax.fori_loop(0, GROUPS, turn, 0)
    g1[dp] = g1_buf[...]
    other_dp(lambda r: to_dp(S_G1, r, g1_buf, g1.at[dp]).start())

    sums[...] = jnp.zeros_like(sums)

    def slots(j, carry):
        sums[...] += lax.dot_general(
            d_pad[rows(j * 256, SUMS)],
            n_pad[rows(PAD + j * 256, 256)],
            (((1,), (1,)), ((), ())),
            preferred_element_type=F32,
        )
        return carry

    lax.fori_loop(0, GROUPS, slots, 0)
    for i in range(far_rows):
        for s in range(NSTR):
            col = jnp.broadcast_to(cols[s : s + 1, BAND + i : BAND + i + 1], (BLOCK, WIDTH))
            block = n_pad[PAD : PAD + BLOCK].astype(F32)
            for c in range(1, i + 1):
                other = n_pad[PAD + c * BLOCK : PAD + (c + 1) * BLOCK].astype(F32)
                block = jnp.where(col == c, other, block)
            picked[i, s * BLOCK : (s + 1) * BLOCK] = block.astype(BF16)
    far = jnp.zeros((BLOCK, 2 * BLOCK), F32)
    for i in range(far_rows):
        far += lax.dot_general(
            d_pad[(BAND + i) * BLOCK : (BAND + i + 1) * BLOCK],
            picked[i],
            (((1,), (1,)), ((), ())),
            preferred_element_type=F32,
        )
    for k in range(SLOTS):
        if k < BAND:
            grad_k = (
                sums[k * BLOCK : (k + 1) * BLOCK, :BLOCK]
                + sums[(k + 1) * BLOCK : (k + 2) * BLOCK, BLOCK:]
            )
        else:
            grad_k = far[:, (k - BAND) * BLOCK : (k - BAND + 1) * BLOCK]
        if k == 0:
            grad_k = jnp.where(lower, grad_k, 0.0)
        slot_buf[k * BLOCK : (k + 1) * BLOCK] = grad_k.astype(BF16)
    mine, theirs = rows(core * HALF, HALF), rows((1 - core) * HALF, HALF)
    swap = to_core(S_R0, slot_buf.at[theirs], r0)
    swap.start()
    swap.wait_recv()
    half_buf[...] = (slot_buf[mine].astype(F32) + r0[...].astype(F32)).astype(BF16)

    def z_rows(r):
        return rows(((z + r) % DEPTH) * PIECE, PIECE)

    for summed, r in weave(range(1, DEPTH), range(BACK_FIRST, SEQ - 1)):
        if summed:
            to_z(S_R1, r, half_buf.at[z_rows(r)], r1.at[z]).start()
        else:
            send_back(r)
    r1[z] = half_buf[z_rows(0)]

    bias_t = bias[...].T
    two = 2 * BLOCK
    far_w = jnp.concatenate([weights[BAND], weights[BAND + 1]], axis=1)
    for i in range(GROUPS):
        out = jnp.dot(band[...], n_pad[i * two : i * two + SPAN], preferred_element_type=F32)
        for h in range(2):
            half = out[h * BLOCK : (h + 1) * BLOCK]
            b = 2 * i + h
            if b >= BAND:
                half += jnp.dot(far_w, picked[b - BAND], preferred_element_type=F32)
            half += bias_t[:, b : b + 1]
            mx_all[b * BLOCK : (b + 1) * BLOCK] = half.astype(BF16)

    def send_mixed(r):
        to_seq(S_MX, r, mx_all.at[rows(ahead(r) * TOK, TOK)], mx_back.at[sq]).start()

    other_dp(lambda r: from_dp(S_G1, r, g1.at[(dp + DP - r) % DP]))
    total = jnp.sum(jnp.sum(g1[...], axis=0), axis=0, keepdims=True)
    my_gain = gain[:, lanes(sq * WIDTH, WIDTH)]
    g2[sq] = jnp.broadcast_to(total / (my_gain * math.sqrt(DP * TOTAL)), (8, WIDTH))
    for r in range(SEQ - 1):
        to_seq(S_G2, r, g2.at[sq], g2.at[sq]).start()

    for r in range(1, DEPTH):
        from_z(S_R1, r, r1.at[(z + DEPTH - r) % DEPTH])

    def sum_piece(t, carry):
        part[t] = jnp.sum(r1[:, rows(t * SUB, SUB), :].astype(F32), axis=0)
        return carry

    lax.fori_loop(0, REDUCERS, sum_piece, 0)
    for r in range(SEQ - 1):
        @pl.when(ahead(r) < REDUCERS)
        def _():
            to_seq(S_R2, r, part.at[ahead(r)], r2.at[sq]).start()

    for r in range(MIX_FIRST):
        send_mixed(r)

    @pl.when(sq < REDUCERS)
    def _():
        r2[sq] = part[sq]
        for r in range(SEQ - 1):
            from_seq(S_R2, r, r2.at[behind(r)])
        r2b[sq] = jnp.sum(r2[...], axis=0)
        for r in range(SEQ - 1):
            to_seq(S_R2B, r, r2b.at[sq], r2b.at[sq]).start()

    for r in range(MIX_FIRST, MIX_SECOND):
        send_mixed(r)
    mx_back[sq] = mx_all[my_rows]

    for r in range(SEQ - 1):
        @pl.when(behind(r) < REDUCERS)
        def _():
            from_seq(S_R2B, r, r2b.at[behind(r)])

    for t in range(REDUCERS):
        r3_buf[t * SUB : (t + 1) * SUB] = r2b[t].astype(BF16)
    my_piece = core * DEPTH + z
    for summed, r in weave(range(1, DEPTH), range(MIX_SECOND, SEQ - 1)):
        if summed:
            to_z(S_R3, r, r3_buf, r3.at[my_piece]).start()
        else:
            send_mixed(r)
    r3[my_piece] = r3_buf[...]

    for r in range(SEQ - 1):
        from_seq(S_DN, r, dn_back.at[behind(r)])

    def value_rows(c, carry):
        at = rows(c * CHUNK, CHUNK)
        first = jnp.zeros((CHUNK, WIDTH), F32)
        second = jnp.zeros((CHUNK, WIDTH), F32)
        for p in range(SEQ):
            cut = slice(p * WIDTH, (p + 1) * WIDTH)
            hat_grad = dn_back[p, at].astype(F32) * gain[:, cut]
            first += hat_grad
            second += hat_grad * hat_ref[at, cut]
        mean1 = jnp.sum(first, axis=1, keepdims=True) * (1.0 / FEAT)
        mean2 = jnp.sum(second, axis=1, keepdims=True) * (1.0 / FEAT)
        inv = inv_ref[at][:, :1]
        for p in range(SEQ):
            cut = slice(p * WIDTH, (p + 1) * WIDTH)
            hat_grad = dn_back[p, at].astype(F32) * gain[:, cut]
            out = inv * (hat_grad - mean1 - hat_ref[at, cut] * mean2)
            value_grad[at, cut] = out.astype(BF16)
        return carry

    lax.fori_loop(0, TOK // CHUNK, value_rows, 0)

    other_dp(lambda r: from_dp(S_BIAS, r, bias_all.at[(dp + DP - r) % DP]))
    bias_sum = jnp.sum(jnp.sum(bias_all[...], axis=0), axis=0, keepdims=True)
    bias_grad[...] = bias_sum * (1.0 / math.sqrt(DP * FEAT))
    for r in range(SEQ - 1):
        from_seq(S_G2, r, g2.at[behind(r)])
    for p in range(SEQ):
        gain_grad[:, p * WIDTH : (p + 1) * WIDTH] = g2[p, :1]

    def finish(panel):
        at = lanes(panel * WIDTH, WIDTH)
        gated_grad[:, at] = (g_ref[:, at].astype(F32) * mx_back[panel].astype(F32)).astype(BF16)

    finish(sq)
    for r in range(7):
        from_seq(S_MX, r, mx_back.at[behind(r)])
        finish(behind(r))

    for r in range(1, DEPTH):
        from_z(S_R3, r, r3.at[core * DEPTH + (z + DEPTH - r) % DEPTH])
    half = r3.at[pl.ds(core * DEPTH, DEPTH)]
    pass_on = to_core(S_R4, half, half)
    pass_on.start()
    scale = 1.0 / math.sqrt(DP * TOTAL * FEAT)

    def scale_half(which):
        for t in range(DEPTH):
            piece = which * DEPTH + t
            weight_grad[rows(piece * PIECE, PIECE)] = r3[piece].astype(F32) * scale

    scale_half(core)
    for r in range(7, SEQ - 1):
        from_seq(S_MX, r, mx_back.at[behind(r)])
        finish(behind(r))
    other = r3.at[pl.ds((1 - core) * DEPTH, DEPTH)]
    to_core(S_R4, other, other).wait_recv()
    scale_half(1 - core)

    for r in range(SEQ - 1):
        to_seq(S_D, r, d_buf.at[ahead(r)], d_pad.at[my_rows]).wait_send()
        to_seq(S_N, r, n_buf.at[ahead(r)], n_pad.at[my_padded]).wait_send()
        to_seq(S_DN, r, dn_all.at[rows(ahead(r) * TOK, TOK)], dn_back.at[sq]).wait_send()
        to_seq(S_MX, r, mx_all.at[rows(ahead(r) * TOK, TOK)], mx_back.at[sq]).wait_send()
        to_seq(S_G2, r, g2.at[sq], g2.at[sq]).wait_send()

        @pl.when(ahead(r) < REDUCERS)
        def _():
            to_seq(S_R2, r, part.at[ahead(r)], r2.at[sq]).wait_send()

        @pl.when(sq < REDUCERS)
        def _():
            to_seq(S_R2B, r, r2b.at[sq], r2b.at[sq]).wait_send()

    def sent(r):
        to_dp(S_BIAS, r, bias_all.at[dp], bias_all.at[dp]).wait_send()
        to_dp(S_G1, r, g1_buf, g1.at[dp]).wait_send()
    other_dp(sent)
    swap.wait_send()
    pass_on.wait_send()
    for r in range(1, DEPTH):
        to_z(S_R1, r, half_buf.at[z_rows(r)], r1.at[z]).wait_send()
        to_z(S_R3, r, r3_buf, r3.at[my_piece]).wait_send()


def shards(gated_part, mixed_part, out_grad, norm_gain, mix_bias, token_mixing_weight, stride_cols):
    vmem = pl.BlockSpec(memory_space=pltpu.VMEM)
    hbm = pl.BlockSpec(memory_space=pltpu.HBM)
    wide = (TOK, FEAT)
    panels = (SEQ, TOK, WIDTH)
    scratch = [
        (wide, BF16), (wide, BF16), (wide, BF16), ((1, FEAT), F32), ((TOTAL // BLOCK, BLOCK), F32),
        ((SLOTS, BLOCK, BLOCK), BF16), ((NSTR, TOTAL // BLOCK), jnp.int32), (wide, F32), ((TOK, BLOCK), F32),
        (panels, BF16), (panels, BF16),
        ((TOTAL + PAD + BLOCK, WIDTH), BF16), ((TOTAL + PAD, WIDTH), BF16),
        ((TOTAL, WIDTH), BF16), ((TOTAL, WIDTH), BF16), (panels, BF16), (panels, BF16),
        ((2 * BLOCK, SPAN), BF16), ((2 * BLOCK, SPAN), BF16), ((8 * BLOCK, 8 * BLOCK), BF16),
        ((NSTR, BLOCK, BLOCK), F32), ((8, NSTR * BLOCK, WIDTH), BF16),
        ((SUMS, 256), F32), ((SLOTS * BLOCK, BLOCK), BF16),
        ((HALF, BLOCK), BF16), ((HALF, BLOCK), BF16),
        ((DEPTH, PIECE, BLOCK), BF16), ((REDUCERS, SUB, BLOCK), F32), ((SEQ, SUB, BLOCK), F32),
        ((REDUCERS, SUB, BLOCK), F32), ((PIECE, BLOCK), BF16), ((DP, PIECE, BLOCK), BF16),
        ((TOK, BLOCK), F32), ((DP, 8, TOK), F32),
        ((8, WIDTH), F32), ((DP, 8, WIDTH), F32), ((SEQ, 8, WIDTH), F32),
    ]
    outs = pl.pallas_call(
        kernel,
        out_shape=(
            jax.ShapeDtypeStruct(wide, BF16),
            jax.ShapeDtypeStruct(wide, BF16),
            jax.ShapeDtypeStruct((SLOTS * BLOCK, BLOCK), F32),
            jax.ShapeDtypeStruct((1, FEAT), F32),
            jax.ShapeDtypeStruct((1, TOK), F32),
        ),
        in_specs=[hbm] * 7,
        out_specs=[vmem] * 5,
        scratch_shapes=[pltpu.VMEM(shape, kind) for shape, kind in scratch]
        + [
            pltpu.SemaphoreType.DMA((7,)),
            pltpu.SemaphoreType.DMA((PHASES, SEQ)),
            pltpu.SemaphoreType.DMA((PHASES, SEQ)),
        ],
        compiler_params=pltpu.CompilerParams(
            collective_id=0, has_side_effects=True, vmem_limit_bytes=56 * 2**20
        ),
    )(
        gated_part[0],
        mixed_part[0],
        out_grad[0],
        norm_gain.reshape(1, FEAT),
        mix_bias.reshape(TOTAL // BLOCK, BLOCK),
        token_mixing_weight,
        stride_cols.T,
    )
    gated_grad, value_grad, weight_grad, gain_grad, bias_grad = outs
    return (
        gated_grad[None],
        value_grad[None],
        weight_grad.reshape(SLOTS, BLOCK, BLOCK),
        gain_grad.reshape(FEAT),
        bias_grad.reshape(TOK),
    )


def solution(mesh):
    placed = (P("dp", "seq", None), P("dp", "seq", None), P("dp", "seq", None), P(), P(), P(), P())
    return jax.shard_map(
        shards,
        mesh=mesh,
        in_specs=placed,
        out_specs=(P("dp", "seq", None), P("dp", "seq", None), P(), P(), P("seq")),
        check_vma=False,
    )
```

```python
import math

import jax
import jax.numpy as jnp
from jax import lax
from jax.experimental import pallas as pl
from jax.experimental.pallas import tpu as pltpu
from jax.sharding import PartitionSpec as P

BLOCK = 128
BAND = 16
NSTR = 2
EPS = 1e-05
MESH = pl.DeviceIdType.MESH
F32 = jnp.float32
BF16 = jnp.bfloat16

OFFSETS = (
    (2, 2), (1, 2), (2, 1), (3, 2), (2, 3), (1, 1), (3, 3), (1, 3),
    (3, 1), (0, 2), (2, 0), (0, 1), (1, 0), (0, 3), (3, 0),
)

SEQ = 16
DP = 16
TOK = 192
FEAT = 4096
WIDTH = FEAT // SEQ
TOTAL = TOK * SEQ
GROUPS = TOTAL // (2 * BLOCK)
SPAN = (BAND + 1) * BLOCK
PAD = (BAND - 1) * BLOCK
SUMS = (BAND + 2) * BLOCK
SLOTS = BAND + NSTR
PIECE = SLOTS * BLOCK // DP
SUB = 16
DEPTH = 8
HALF = DEPTH * PIECE
REDUCERS = PIECE // SUB
CHUNK = 16

S_D, S_N, S_DN, S_MX, S_R1, S_R2, S_R2B, S_R3, S_BIAS, S_G1, S_G2, S_R0, S_R4 = range(13)
PHASES = 13
BACK_FIRST = 9
MIX_FIRST = 0
MIX_SECOND = 2


def weave(first, second):
    order = []
    for i, item in enumerate(first):
        order.append((True, item))
        order += [(False, other) for q, other in enumerate(second) if q * len(first) // len(second) == i]
    return order


def rows(start, size):
    return pl.ds(pl.multiple_of(start, 16), size)


def lanes(start, size):
    return pl.ds(pl.multiple_of(start, 128), size)


def kernel(
    gated, value, grad, gain_in, bias_in, weights_in, cols_in,
    gated_grad, value_grad, weight_grad, gain_grad, bias_grad,
    u_ref, v_ref, g_ref, gain, bias, weights, cols, hat_ref, inv_ref,
    d_buf, n_buf, d_pad, n_pad, dn_all, mx_all, dn_back, mx_back,
    band, band_t, corner_t, wt_ref, picked, sums, slot_buf,
    r0, half_buf, r1, part, r2, r2b, r3_buf, r3, bias_acc, bias_all, g1_buf, g1, g2,
    in_sem, ss, rs,
):
    dp = lax.axis_index("dp")
    sq = lax.axis_index("seq")
    x, y = sq // 4, sq % 4
    z, core = dp // 2, dp % 2

    def ahead(r):
        dx, dy = OFFSETS[r]
        return ((x + dx) % 4) * 4 + (y + dy) % 4

    def behind(r):
        dx, dy = OFFSETS[r]
        return ((x + 4 - dx) % 4) * 4 + (y + 4 - dy) % 4

    def to_seq(phase, r, src, dst):
        return pltpu.make_async_remote_copy(
            src_ref=src, dst_ref=dst, send_sem=ss.at[phase, r], recv_sem=rs.at[phase, r],
            device_id=(dp, ahead(r)), device_id_type=MESH,
        )

    def from_seq(phase, r, slot):
        pltpu.make_async_remote_copy(
            src_ref=slot, dst_ref=slot, send_sem=ss.at[phase, r], recv_sem=rs.at[phase, r],
            device_id=(dp, behind(r)), device_id_type=MESH,
        ).wait_recv()

    def to_dp(phase, r, src, dst):
        return pltpu.make_async_remote_copy(
            src_ref=src, dst_ref=dst, send_sem=ss.at[phase, r], recv_sem=rs.at[phase, r],
            device_id=((dp + r) % DP, sq), device_id_type=MESH,
        )

    def from_dp(phase, r, slot):
        pltpu.make_async_remote_copy(
            src_ref=slot, dst_ref=slot, send_sem=ss.at[phase, r], recv_sem=rs.at[phase, r],
            device_id=((dp + DP - r) % DP, sq), device_id_type=MESH,
        ).wait_recv()

    def to_z(phase, r, src, dst):
        return pltpu.make_async_remote_copy(
            src_ref=src, dst_ref=dst, send_sem=ss.at[phase, r], recv_sem=rs.at[phase, r],
            device_id=(((z + r) % DEPTH) * 2 + core, sq), device_id_type=MESH,
        )

    def from_z(phase, r, slot):
        pltpu.make_async_remote_copy(
            src_ref=slot, dst_ref=slot, send_sem=ss.at[phase, r], recv_sem=rs.at[phase, r],
            device_id=(((z + DEPTH - r) % DEPTH) * 2 + core, sq), device_id_type=MESH,
        ).wait_recv()

    def to_core(phase, src, dst):
        return pltpu.make_async_remote_copy(
            src_ref=src, dst_ref=dst, send_sem=ss.at[phase, 0], recv_sem=rs.at[phase, 0],
            device_id=(z * 2 + 1 - core, sq), device_id_type=MESH,
        )

    def other_dp(body):
        def step(r, carry):
            body(r)
            return carry

        lax.fori_loop(1, DP, step, 0)

    loads = [
        pltpu.make_async_copy(src, dst, in_sem.at[i])
        for i, (src, dst) in enumerate(
            (
                (grad, g_ref), (gated, u_ref), (value, v_ref), (gain_in, gain),
                (bias_in, bias), (weights_in, weights), (cols_in, cols),
            )
        )
    ]
    for load in loads:
        load.start()

    barrier = pltpu.get_barrier_semaphore()
    for r in range(SEQ - 1):
        pl.semaphore_signal(barrier, inc=1, device_id=(dp, ahead(r)), device_id_type=MESH)
    other_dp(
        lambda r: pl.semaphore_signal(
            barrier, inc=1, device_id=((dp + r) % DP, sq), device_id_type=MESH
        )
    )

    loads[0].wait()
    loads[1].wait()
    bias_acc[...] = jnp.zeros_like(bias_acc)

    def make_d(panel):
        at = lanes(panel * WIDTH, WIDTH)
        d = (g_ref[:, at].astype(F32) * u_ref[:, at].astype(F32)).astype(BF16)
        wide = d.astype(F32)
        bias_acc[...] += wide[:, :BLOCK] + wide[:, BLOCK:]
        return d

    my_rows = rows(sq * TOK, TOK)
    d_buf[ahead(0)] = make_d(ahead(0))
    pl.semaphore_wait(barrier, SEQ - 1 + DP - 1)
    for r in range(SEQ - 1):
        panel = ahead(r)
        if r > 0:
            d_buf[panel] = make_d(panel)
        to_seq(S_D, r, d_buf.at[panel], d_pad.at[my_rows]).start()
    d_pad[my_rows] = make_d(sq)

    for load in loads[2:]:
        load.wait()

    def norm_rows(c, carry):
        at = rows(c * CHUNK, CHUNK)
        total = jnp.zeros((CHUNK, WIDTH), F32)
        for p in range(SEQ):
            total += v_ref[at, p * WIDTH : (p + 1) * WIDTH].astype(F32)
        mean = jnp.sum(total, axis=1, keepdims=True) * (1.0 / FEAT)
        total = jnp.zeros((CHUNK, WIDTH), F32)
        for p in range(SEQ):
            centered = v_ref[at, p * WIDTH : (p + 1) * WIDTH].astype(F32) - mean
            total += centered * centered
        inv = lax.rsqrt(jnp.sum(total, axis=1, keepdims=True) * (1.0 / FEAT) + EPS)
        inv_ref[at] = jnp.broadcast_to(inv, (CHUNK, BLOCK))
        for p in range(SEQ):
            cut = slice(p * WIDTH, (p + 1) * WIDTH)
            hat = (v_ref[at, cut].astype(F32) - mean) * inv
            hat_ref[at, cut] = hat
            n_buf[p, at] = (hat * gain[:, cut]).astype(BF16)
        return carry

    lax.fori_loop(0, TOK // CHUNK, norm_rows, 0)
    my_padded = rows(PAD + sq * TOK, TOK)
    for r in range(SEQ - 1):
        to_seq(S_N, r, n_buf.at[ahead(r)], n_pad.at[my_padded]).start()
    n_pad[my_padded] = n_buf[sq]

    part_bias = bias_acc[...].T.reshape(BLOCK // 8, 8, TOK)
    bias_all[dp] = jnp.sum(part_bias, axis=0)
    other_dp(lambda r: to_dp(S_BIAS, r, bias_all.at[dp], bias_all.at[dp]).start())

    zero_block = jnp.zeros((BLOCK, BLOCK), BF16)
    row_ids = lax.broadcasted_iota(jnp.int32, (BLOCK, BLOCK), 0)
    col_ids = lax.broadcasted_iota(jnp.int32, (BLOCK, BLOCK), 1)
    lower = row_ids >= col_ids
    for i, m in ((0, BAND), (1, 0)):
        for matrix in (band, band_t):
            matrix[i * BLOCK : (i + 1) * BLOCK, m * BLOCK : (m + 1) * BLOCK] = zero_block
    for k in range(SLOTS):
        w32 = weights[k].astype(F32)
        if k == 0:
            w32 = jnp.where(lower, w32, 0.0)
        w = w32.astype(BF16)
        wt32 = w32.T
        wt = wt32.astype(BF16)
        if k < BAND:
            for i in range(2):
                at = slice(i * BLOCK, (i + 1) * BLOCK)
                m = i + BAND - 1 - k
                band[at, m * BLOCK : (m + 1) * BLOCK] = w
                m = i + k
                band_t[at, m * BLOCK : (m + 1) * BLOCK] = wt
        else:
            wt_ref[k - BAND] = wt32

    far_rows = GROUPS * 2 - BAND

    def corner_row(j, carry):
        for i in range(far_rows):
            block = jnp.zeros((BLOCK, BLOCK), F32)
            for s in range(NSTR):
                hit = jnp.broadcast_to(cols[s : s + 1, BAND + i : BAND + i + 1], (BLOCK, BLOCK)) == j
                block += jnp.where(hit, wt_ref[s], 0.0)
            corner_t[rows(j * BLOCK, BLOCK), i * BLOCK : (i + 1) * BLOCK] = block.astype(BF16)
        return carry

    lax.fori_loop(0, far_rows, corner_row, 0)
    d_pad[TOTAL:] = jnp.zeros((PAD + BLOCK, WIDTH), BF16)
    n_pad[:PAD] = jnp.zeros((PAD, WIDTH), BF16)

    for r in range(SEQ - 1):
        from_seq(S_D, r, d_pad.at[rows(behind(r) * TOK, TOK)])

    def back_near(j, carry):
        out = jnp.dot(band_t[...], d_pad[rows(j * 256, SPAN)], preferred_element_type=F32)
        dn_all[rows(j * 256, 256)] = out.astype(BF16)
        return carry

    def back_far(j, carry):
        out = jnp.dot(band_t[...], d_pad[rows(j * 256, SPAN)], preferred_element_type=F32)
        out += jnp.dot(
            corner_t[rows(j * 256, 256)], d_pad[BAND * BLOCK : TOTAL], preferred_element_type=F32
        )
        dn_all[rows(j * 256, 256)] = out.astype(BF16)
        return carry

    lax.fori_loop(0, far_rows // 2, back_far, 0)
    lax.fori_loop(far_rows // 2, GROUPS, back_near, 0)

    def send_back(r):
        to_seq(S_DN, r, dn_all.at[rows(ahead(r) * TOK, TOK)], dn_back.at[sq]).start()

    for r in range(BACK_FIRST):
        send_back(r)
    dn_back[sq] = dn_all[my_rows]

    for r in range(SEQ - 1):
        from_seq(S_N, r, n_pad.at[rows(PAD + behind(r) * TOK, TOK)])

    g1_buf[...] = jnp.zeros_like(g1_buf)

    def turn(i, carry):
        wide = n_pad[rows(PAD + i * 256, 256)].astype(F32)
        dn = dn_all[rows(i * 256, 256)].astype(F32)
        g1_buf[...] += jnp.sum((dn * wide).reshape(32, 8, WIDTH), axis=0)
        return carry

    lax.fori_loop(0, GROUPS, turn, 0)
    g1[dp] = g1_buf[...]
    other_dp(lambda r: to_dp(S_G1, r, g1_buf, g1.at[dp]).start())

    sums[...] = jnp.zeros_like(sums)

    def slots(j, carry):
        sums[...] += lax.dot_general(
            d_pad[rows(j * 256, SUMS)],
            n_pad[rows(PAD + j * 256, 256)],
            (((1,), (1,)), ((), ())),
            preferred_element_type=F32,
        )
        return carry

    lax.fori_loop(0, GROUPS, slots, 0)
    for i in range(far_rows):
        for s in range(NSTR):
            col = jnp.broadcast_to(cols[s : s + 1, BAND + i : BAND + i + 1], (BLOCK, WIDTH))
            block = n_pad[PAD : PAD + BLOCK].astype(F32)
            for c in range(1, i + 1):
                other = n_pad[PAD + c * BLOCK : PAD + (c + 1) * BLOCK].astype(F32)
                block = jnp.where(col == c, other, block)
            picked[i, s * BLOCK : (s + 1) * BLOCK] = block.astype(BF16)
    far = jnp.zeros((BLOCK, 2 * BLOCK), F32)
    for i in range(far_rows):
        far += lax.dot_general(
            d_pad[(BAND + i) * BLOCK : (BAND + i + 1) * BLOCK],
            picked[i],
            (((1,), (1,)), ((), ())),
            preferred_element_type=F32,
        )
    for k in range(SLOTS):
        if k < BAND:
            grad_k = (
                sums[k * BLOCK : (k + 1) * BLOCK, :BLOCK]
                + sums[(k + 1) * BLOCK : (k + 2) * BLOCK, BLOCK:]
            )
        else:
            grad_k = far[:, (k - BAND) * BLOCK : (k - BAND + 1) * BLOCK]
        if k == 0:
            grad_k = jnp.where(lower, grad_k, 0.0)
        slot_buf[k * BLOCK : (k + 1) * BLOCK] = grad_k.astype(BF16)
    mine, theirs = rows(core * HALF, HALF), rows((1 - core) * HALF, HALF)
    swap = to_core(S_R0, slot_buf.at[theirs], r0)
    swap.start()
    swap.wait_recv()
    half_buf[...] = (slot_buf[mine].astype(F32) + r0[...].astype(F32)).astype(BF16)

    def z_rows(r):
        return rows(((z + r) % DEPTH) * PIECE, PIECE)

    for summed, r in weave(range(1, DEPTH), range(BACK_FIRST, SEQ - 1)):
        if summed:
            to_z(S_R1, r, half_buf.at[z_rows(r)], r1.at[z]).start()
        else:
            send_back(r)
    r1[z] = half_buf[z_rows(0)]

    bias_t = bias[...].T
    two = 2 * BLOCK
    far_w = jnp.concatenate([weights[BAND], weights[BAND + 1]], axis=1)
    for i in range(GROUPS):
        out = jnp.dot(band[...], n_pad[i * two : i * two + SPAN], preferred_element_type=F32)
        for h in range(2):
            half = out[h * BLOCK : (h + 1) * BLOCK]
            b = 2 * i + h
            if b >= BAND:
                half += jnp.dot(far_w, picked[b - BAND], preferred_element_type=F32)
            half += bias_t[:, b : b + 1]
            mx_all[b * BLOCK : (b + 1) * BLOCK] = half.astype(BF16)

    def send_mixed(r):
        to_seq(S_MX, r, mx_all.at[rows(ahead(r) * TOK, TOK)], mx_back.at[sq]).start()

    other_dp(lambda r: from_dp(S_G1, r, g1.at[(dp + DP - r) % DP]))
    total = jnp.sum(jnp.sum(g1[...], axis=0), axis=0, keepdims=True)
    my_gain = gain[:, lanes(sq * WIDTH, WIDTH)]
    g2[sq] = jnp.broadcast_to(total / (my_gain * math.sqrt(DP * TOTAL)), (8, WIDTH))
    for r in range(SEQ - 1):
        to_seq(S_G2, r, g2.at[sq], g2.at[sq]).start()

    for r in range(1, DEPTH):
        from_z(S_R1, r, r1.at[(z + DEPTH - r) % DEPTH])

    def sum_piece(t, carry):
        part[t] = jnp.sum(r1[:, rows(t * SUB, SUB), :].astype(F32), axis=0)
        return carry

    lax.fori_loop(0, REDUCERS, sum_piece, 0)
    for r in range(SEQ - 1):
        @pl.when(ahead(r) < REDUCERS)
        def _():
            to_seq(S_R2, r, part.at[ahead(r)], r2.at[sq]).start()

    for r in range(MIX_FIRST):
        send_mixed(r)

    @pl.when(sq < REDUCERS)
    def _():
        r2[sq] = part[sq]
        for r in range(SEQ - 1):
            from_seq(S_R2, r, r2.at[behind(r)])
        r2b[sq] = jnp.sum(r2[...], axis=0)
        for r in range(SEQ - 1):
            to_seq(S_R2B, r, r2b.at[sq], r2b.at[sq]).start()

    for r in range(MIX_FIRST, MIX_SECOND):
        send_mixed(r)
    mx_back[sq] = mx_all[my_rows]

    for r in range(SEQ - 1):
        @pl.when(behind(r) < REDUCERS)
        def _():
            from_seq(S_R2B, r, r2b.at[behind(r)])

    for t in range(REDUCERS):
        r3_buf[t * SUB : (t + 1) * SUB] = r2b[t].astype(BF16)
    my_piece = core * DEPTH + z
    for summed, r in weave(range(1, DEPTH), range(MIX_SECOND, SEQ - 1)):
        if summed:
            to_z(S_R3, r, r3_buf, r3.at[my_piece]).start()
        else:
            send_mixed(r)
    r3[my_piece] = r3_buf[...]

    for r in range(SEQ - 1):
        from_seq(S_DN, r, dn_back.at[behind(r)])

    def value_rows(c, carry):
        at = rows(c * CHUNK, CHUNK)
        first = jnp.zeros((CHUNK, WIDTH), F32)
        second = jnp.zeros((CHUNK, WIDTH), F32)
        for p in range(SEQ):
            cut = slice(p * WIDTH, (p + 1) * WIDTH)
            hat_grad = dn_back[p, at].astype(F32) * gain[:, cut]
            first += hat_grad
            second += hat_grad * hat_ref[at, cut]
        mean1 = jnp.sum(first, axis=1, keepdims=True) * (1.0 / FEAT)
        mean2 = jnp.sum(second, axis=1, keepdims=True) * (1.0 / FEAT)
        inv = inv_ref[at][:, :1]
        for p in range(SEQ):
            cut = slice(p * WIDTH, (p + 1) * WIDTH)
            hat_grad = dn_back[p, at].astype(F32) * gain[:, cut]
            out = inv * (hat_grad - mean1 - hat_ref[at, cut] * mean2)
            value_grad[at, cut] = out.astype(BF16)
        return carry

    lax.fori_loop(0, TOK // CHUNK, value_rows, 0)

    other_dp(lambda r: from_dp(S_BIAS, r, bias_all.at[(dp + DP - r) % DP]))
    bias_sum = jnp.sum(jnp.sum(bias_all[...], axis=0), axis=0, keepdims=True)
    bias_grad[...] = bias_sum * (1.0 / math.sqrt(DP * FEAT))
    for r in range(SEQ - 1):
        from_seq(S_G2, r, g2.at[behind(r)])
    for p in range(SEQ):
        gain_grad[:, p * WIDTH : (p + 1) * WIDTH] = g2[p, :1]

    def finish(panel):
        at = lanes(panel * WIDTH, WIDTH)
        gated_grad[:, at] = (g_ref[:, at].astype(F32) * mx_back[panel].astype(F32)).astype(BF16)

    finish(sq)
    for r in range(7):
        from_seq(S_MX, r, mx_back.at[behind(r)])
        finish(behind(r))

    for r in range(1, DEPTH):
        from_z(S_R3, r, r3.at[core * DEPTH + (z + DEPTH - r) % DEPTH])
    half = r3.at[pl.ds(core * DEPTH, DEPTH)]
    pass_on = to_core(S_R4, half, half)
    pass_on.start()
    scale = 1.0 / math.sqrt(DP * TOTAL * FEAT)

    def scale_half(which):
        for t in range(DEPTH):
            piece = which * DEPTH + t
            weight_grad[rows(piece * PIECE, PIECE)] = r3[piece].astype(F32) * scale

    scale_half(core)
    for r in range(7, SEQ - 1):
        from_seq(S_MX, r, mx_back.at[behind(r)])
        finish(behind(r))
    other = r3.at[pl.ds((1 - core) * DEPTH, DEPTH)]
    to_core(S_R4, other, other).wait_recv()
    scale_half(1 - core)

    for r in range(SEQ - 1):
        to_seq(S_D, r, d_buf.at[ahead(r)], d_pad.at[my_rows]).wait_send()
        to_seq(S_N, r, n_buf.at[ahead(r)], n_pad.at[my_padded]).wait_send()
        to_seq(S_DN, r, dn_all.at[rows(ahead(r) * TOK, TOK)], dn_back.at[sq]).wait_send()
        to_seq(S_MX, r, mx_all.at[rows(ahead(r) * TOK, TOK)], mx_back.at[sq]).wait_send()
        to_seq(S_G2, r, g2.at[sq], g2.at[sq]).wait_send()

        @pl.when(ahead(r) < REDUCERS)
        def _():
            to_seq(S_R2, r, part.at[ahead(r)], r2.at[sq]).wait_send()

        @pl.when(sq < REDUCERS)
        def _():
            to_seq(S_R2B, r, r2b.at[sq], r2b.at[sq]).wait_send()

    def sent(r):
        to_dp(S_BIAS, r, bias_all.at[dp], bias_all.at[dp]).wait_send()
        to_dp(S_G1, r, g1_buf, g1.at[dp]).wait_send()
    other_dp(sent)
    swap.wait_send()
    pass_on.wait_send()
    for r in range(1, DEPTH):
        to_z(S_R1, r, half_buf.at[z_rows(r)], r1.at[z]).wait_send()
        to_z(S_R3, r, r3_buf, r3.at[my_piece]).wait_send()


def shards(gated_part, mixed_part, out_grad, norm_gain, mix_bias, token_mixing_weight, stride_cols):
    vmem = pl.BlockSpec(memory_space=pltpu.VMEM)
    hbm = pl.BlockSpec(memory_space=pltpu.HBM)
    wide = (TOK, FEAT)
    panels = (SEQ, TOK, WIDTH)
    scratch = [
        (wide, BF16), (wide, BF16), (wide, BF16), ((1, FEAT), F32), ((TOTAL // BLOCK, BLOCK), F32),
        ((SLOTS, BLOCK, BLOCK), BF16), ((NSTR, TOTAL // BLOCK), jnp.int32), (wide, F32), ((TOK, BLOCK), F32),
        (panels, BF16), (panels, BF16),
        ((TOTAL + PAD + BLOCK, WIDTH), BF16), ((TOTAL + PAD, WIDTH), BF16),
        ((TOTAL, WIDTH), BF16), ((TOTAL, WIDTH), BF16), (panels, BF16), (panels, BF16),
        ((2 * BLOCK, SPAN), BF16), ((2 * BLOCK, SPAN), BF16), ((8 * BLOCK, 8 * BLOCK), BF16),
        ((NSTR, BLOCK, BLOCK), F32), ((8, NSTR * BLOCK, WIDTH), BF16),
        ((SUMS, 256), F32), ((SLOTS * BLOCK, BLOCK), BF16),
        ((HALF, BLOCK), BF16), ((HALF, BLOCK), BF16),
        ((DEPTH, PIECE, BLOCK), BF16), ((REDUCERS, SUB, BLOCK), F32), ((SEQ, SUB, BLOCK), F32),
        ((REDUCERS, SUB, BLOCK), F32), ((PIECE, BLOCK), BF16), ((DP, PIECE, BLOCK), BF16),
        ((TOK, BLOCK), F32), ((DP, 8, TOK), F32),
        ((8, WIDTH), F32), ((DP, 8, WIDTH), F32), ((SEQ, 8, WIDTH), F32),
    ]
    outs = pl.pallas_call(
        kernel,
        out_shape=(
            jax.ShapeDtypeStruct(wide, BF16),
            jax.ShapeDtypeStruct(wide, BF16),
            jax.ShapeDtypeStruct((SLOTS * BLOCK, BLOCK), F32),
            jax.ShapeDtypeStruct((1, FEAT), F32),
            jax.ShapeDtypeStruct((1, TOK), F32),
        ),
        in_specs=[hbm] * 7,
        out_specs=[vmem] * 5,
        scratch_shapes=[pltpu.VMEM(shape, kind) for shape, kind in scratch]
        + [
            pltpu.SemaphoreType.DMA((7,)),
            pltpu.SemaphoreType.DMA((PHASES, SEQ)),
            pltpu.SemaphoreType.DMA((PHASES, SEQ)),
        ],
        compiler_params=pltpu.CompilerParams(
            collective_id=0, has_side_effects=True, vmem_limit_bytes=56 * 2**20
        ),
    )(
        gated_part[0],
        mixed_part[0],
        out_grad[0],
        norm_gain.reshape(1, FEAT),
        mix_bias.reshape(TOTAL // BLOCK, BLOCK),
        token_mixing_weight,
        stride_cols.T,
    )
    gated_grad, value_grad, weight_grad, gain_grad, bias_grad = outs
    return (
        gated_grad[None],
        value_grad[None],
        weight_grad.reshape(SLOTS, BLOCK, BLOCK),
        gain_grad.reshape(FEAT),
        bias_grad.reshape(TOK),
    )


def solution(mesh):
    placed = (P("dp", "seq", None), P("dp", "seq", None), P("dp", "seq", None), P(), P(), P(), P())
    return jax.shard_map(
        shards,
        mesh=mesh,
        in_specs=placed,
        out_specs=(P("dp", "seq", None), P("dp", "seq", None), P(), P(), P("seq")),
        check_vma=False,
    )
```
